512 devices in a mesh: expert: 2 (over core), branch: 2 (over x_hi), seq: 16 (over z, x_lo), tensor: 8 (over y).
Axes of the slice: x: 4 (x_hi: 2, x_lo: 2; x = x_hi * 2 + x_lo), y: 8, z: 8, core: 2. Of those that a mesh axis runs over, the one named last changes fastest.
Arguments:
- query_raw: bfloat16 [2, 2, 2816, 5120], P('expert', 'branch', 'seq', 'tensor'), may hold values from -40 to 40
- key_raw: bfloat16 [2, 2, 2816, 5120], P('expert', 'branch', 'seq', 'tensor'), may hold values from -40 to 40
- value_rows: bfloat16 [2, 2, 2816, 5120], P('expert', 'branch', 'seq', 'tensor'), may hold values from -6 to 6
- residual: bfloat16 [2, 2, 2816, 5120], P('expert', 'branch', 'seq', 'tensor'), may hold values from -0.8 to 0.8
- latent: float32 [2, 2816, 64], P('expert', 'seq'), may hold values from -6 to 6
- query_gain: float32 [2, 5120], P('expert', 'tensor'), may hold values from 0.7 to 2.8
- key_gain: float32 [2, 5120], P('expert', 'tensor'), may hold values from 0.7 to 2.8
- out_weight: bfloat16 [2, 5120, 5120], P('expert', 'tensor', ('branch', 'seq')), may hold values from -0.078125 to 0.078125
- attn_gate: float32 [2, 5120], P('expert', 'tensor'), may hold values from -2 to 2
- head_shift: float32 [2, 5120], P('expert', 'tensor'), may hold values from -3 to 3
- head_scale: float32 [2, 5120], P('expert', 'tensor'), may hold values from -3 to 3
- head_weight: bfloat16 [2, 5120, 64], P('expert', 'tensor'), may hold values from -0.078125 to 0.078125
- head_bias: float32 [2, 64], P('expert'), may hold values from -3 to 3
- valid_rows: int32 [2], P('expert'), may hold values from 27 to 54
- step_index: int32 [2], P('expert'), may hold values from 0 to 39
Outputs:
- hidden_out: bfloat16 [2, 2, 2816, 5120], P('expert', 'branch', 'seq', 'tensor')
- velocity: float32 [2, 2816, 64], P('expert', 'seq')
- relayed: float32 [2, 2816, 64], P('expert', 'seq')
The draws below stay inside these ranges and needn't reach their ends.
All inputs are finite; a program needn't handle non-finite values.
Results may differ from the reference program's by a relative error of at most 0.011.
The reference program's roundings to bfloat16 on the way count: a program that leaves them out, or rounds other values in their place, can miss the bound.
Values may be sent and summed in bfloat16 or wider, within the bound.
A program may use at most 64 MiB of HBM per device.

```python
import math
import jax
import jax.numpy as jnp
from jax import lax

D = 5120
HEADS = 40
HD = 128
C = 64
GRID_H = 30
GRID_W = 52
STEPS = 40
TOKENS = 2816
ROWS = 54


def column_scales(key):
    rise = jnp.arange(D, dtype=jnp.float32) / D
    return 10.0 ** (0.5 * rise + 0.5 * jax.random.uniform(key, (D,), jnp.float32))


def row_scales(key):
    return 10.0 ** jax.random.uniform(key, (2, 2, TOKENS, 1), jnp.float32)


def base_values(keys, limit_normal):
    column = column_scales(keys[0])
    row = row_scales(keys[1])
    noise = jnp.clip(jax.random.normal(keys[2], (2, 2, TOKENS, D), jnp.float32), -limit_normal, limit_normal)
    return (noise * column[None, None, None, :], row)


def draw_query_raw(key, part):
    key = jax.random.fold_in(key, 1)
    keys = jax.random.split(key, 4)
    scaled, row = base_values(keys, 4.0)
    values = scaled * row / 10.0
    return values.astype(jnp.bfloat16)


def draw_key_raw(key, part):
    key = jax.random.fold_in(key, 2)
    keys = jax.random.split(key, 5)
    scaled, row = base_values(keys, 4.0)
    values = scaled * row / 10.0
    return values.astype(jnp.bfloat16)


def draw_residual(key, part):
    key = jax.random.fold_in(key, 3)
    keys = jax.random.split(key, 4)
    scaled, row = base_values(keys, 3.0)
    return (scaled * row / 400.0).astype(jnp.bfloat16)


def levels(rng, shape, shards, least, top_value):
    factor_of, own = 1.0, jax.random.fold_in(rng, 6)
    for dim, blocks in shards:
        draws = jnp.exp(jax.random.uniform(jax.random.fold_in(own, dim), (blocks,), jnp.float32, least / len(shards), top_value / len(shards)))
        factor_of = factor_of * jnp.repeat(draws, shape[dim] // blocks).reshape([-1 if axis == dim else 1 for axis in range(len(shape))])
    return factor_of


def centred(rng, extent, width, most, cuts=(), kind=jnp.bfloat16):
    values = width * jax.random.normal(rng, extent, jnp.float32)
    if cuts:
        values = values * levels(rng, extent, cuts, -0.22, 0.18)
    return jnp.clip(values, -most, most).astype(kind)


def setup_inputs(seed: int = 0) -> dict:
    key_of = jax.random.split(jax.random.key(seed), 16)
    query_raw = draw_query_raw(jax.random.fold_in(key_of[15], 71), 0)
    key_raw = draw_key_raw(jax.random.fold_in(key_of[15], 71), 0)
    value_rows = centred(key_of[2], (2, 2, TOKENS, D), 1.0, 6.0, ((0, 2), (1, 2), (2, 16), (3, 8)))
    residual = draw_residual(jax.random.fold_in(key_of[15], 71), 0)
    latent = centred(key_of[4], (2, TOKENS, C), 1.0, 6.0, ((0, 2), (1, 16)), jnp.float32)
    query_gain = jnp.clip(jnp.exp(math.log(2.8) - 1.3862944 * jax.random.uniform(key_of[5], (2, D), jnp.float32) ** levels(key_of[5], (2, D), ((0, 2), (1, 8)), -0.2, 0.2)), 0.7, 2.8)
    key_gain = jnp.clip(jnp.exp(math.log(2.8) - 1.3862944 * jax.random.uniform(key_of[6], (2, D), jnp.float32) ** levels(key_of[6], (2, D), ((0, 2), (1, 8)), -0.2, 0.2)), 0.7, 2.8)
    out_weight = centred(key_of[7], (2, D, D), D ** -0.5, 0.078125, ((0, 2), (1, 8), (2, 32)))
    attn_gate = jnp.clip(jax.random.uniform(key_of[8], (2, D), jnp.float32, -2.0, 2.0) * levels(key_of[8], (2, D), ((0, 2), (1, 8)), -0.4, 0.0), -2.0, 2.0)
    head_shift = centred(key_of[9], (2, D), 0.5, 3.0, ((0, 2), (1, 8)), jnp.float32)
    head_scale = centred(key_of[10], (2, D), 0.5, 3.0, ((0, 2), (1, 8)), jnp.float32)
    head_weight = centred(key_of[11], (2, D, C), D ** -0.5, 0.078125, ((0, 2), (1, 8)))
    head_bias = centred(key_of[12], (2, C), 0.5, 3.0, ((0, 2),), jnp.float32)
    valid_rows = jax.random.randint(key_of[13], (2,), max(ROWS // 2, 1), ROWS + 1).astype(jnp.int32)
    step_index = jax.random.randint(key_of[14], (2,), 0, STEPS).astype(jnp.int32)
    return {"query_raw": query_raw, "key_raw": key_raw, "value_rows": value_rows, "residual": residual, "latent": latent, "query_gain": query_gain, "key_gain": key_gain, "out_weight": out_weight, "attn_gate": attn_gate, "head_shift": head_shift, "head_scale": head_scale, "head_weight": head_weight, "head_bias": head_bias, "valid_rows": valid_rows, "step_index": step_index}


EPSILON = 1e-06
THETA = 10000.0
FLOW_SHIFT = 12.0
GUIDE_HIGH = 4.0
GUIDE_LOW = 3.0
MASKED = -1e+30

def rope_tables(positions):
    half_pairs = HD // 2
    third_pairs = half_pairs // 3
    first_pairs = half_pairs - 2 * third_pairs
    frame_tokens = GRID_H * GRID_W
    frame_idx = (positions // frame_tokens).astype(jnp.float32)
    row_idx = (positions % frame_tokens // GRID_W).astype(jnp.float32)
    col_idx = (positions % GRID_W).astype(jnp.float32)
    pair_idx = jnp.arange(half_pairs, dtype=jnp.int32)
    in_time = pair_idx < first_pairs
    in_rows = pair_idx < first_pairs + third_pairs
    log_theta = math.log(THETA)
    rate_time = jnp.exp(-log_theta * pair_idx.astype(jnp.float32) / first_pairs)
    rate_rows = jnp.exp(-log_theta * (pair_idx - first_pairs).astype(jnp.float32) / third_pairs)
    rate_cols = jnp.exp(-log_theta * (pair_idx - first_pairs - third_pairs).astype(jnp.float32) / third_pairs)
    rates = jnp.where(in_time, rate_time, jnp.where(in_rows, rate_rows, rate_cols))
    coords = jnp.where(in_time[None, :], frame_idx[:, None], jnp.where(in_rows[None, :], row_idx[:, None], col_idx[:, None]))
    angles = coords * rates[None, :]
    return (jnp.cos(angles), jnp.sin(angles))

def rotate(values, cosines, sines):
    rows = values.shape[0]
    heads_here = values.shape[1] // HD
    paired = values.reshape(rows, heads_here, HD // 2, 2)
    real_part = paired[..., 0]
    imag_part = paired[..., 1]
    cos_b = cosines[:, None, :]
    sin_b = sines[:, None, :]
    turned = jnp.stack([real_part * cos_b - imag_part * sin_b, real_part * sin_b + imag_part * cos_b], axis=-1)
    return turned.reshape(rows, heads_here * HD)

def normalize_rotate(values, gain, squares, cosines, sines):
    inverse = lax.rsqrt(squares / D + EPSILON)
    return rotate(values * inverse[:, None] * gain[None, :], cosines, sines).astype(jnp.bfloat16)

def attend(queries, keys_rot, values, key_live):
    query_heads = queries.reshape(TOKENS, HEADS, HD).transpose(1, 0, 2)
    key_heads = keys_rot.reshape(TOKENS, HEADS, HD).transpose(1, 0, 2)
    value_heads = values.reshape(TOKENS, HEADS, HD).transpose(1, 0, 2)

    def one_head(operands):
        query_head, key_head, value_head = operands
        logits = jnp.dot(query_head, key_head.T, preferred_element_type=jnp.float32) * HD ** (-0.5)
        logits = jnp.where(key_live[None, :], logits, MASKED)
        peak = lax.optimization_barrier(jnp.max(logits, axis=1, keepdims=True))
        weights = jnp.where(key_live[None, :], jnp.exp(logits - peak), 0.0)
        denom = lax.optimization_barrier(jnp.sum(weights, axis=1, keepdims=True))
        mixed = jnp.dot(weights.astype(jnp.bfloat16), value_head, preferred_element_type=jnp.float32)
        return (mixed / denom).astype(jnp.bfloat16)
    result = lax.map(one_head, (query_heads, key_heads, value_heads))
    return result.transpose(1, 0, 2).reshape(TOKENS, D)

def noise_level(frac):
    return FLOW_SHIFT * frac / (1.0 + (FLOW_SHIFT - 1.0) * frac)

def reference(query_raw, key_raw, value_rows, residual, latent, query_gain, key_gain, out_weight, attn_gate, head_shift, head_scale, head_weight, head_bias, valid_rows, step_index):
    positions = jnp.arange(TOKENS, dtype=jnp.int32)
    cosines, sines = rope_tables(positions)
    hidden_rows = []
    velocities = []
    advanced_rows = []
    for expert_id in range(2):
        key_live = positions < valid_rows[expert_id] * GRID_W
        branch_hidden = []
        branch_velocity = []
        for branch_id in range(2):
            queries = query_raw[expert_id, branch_id].astype(jnp.float32)
            keys_f = key_raw[expert_id, branch_id].astype(jnp.float32)
            query_rot = normalize_rotate(queries, query_gain[expert_id], lax.optimization_barrier(jnp.sum(queries * queries, axis=1)), cosines, sines)
            key_rot = normalize_rotate(keys_f, key_gain[expert_id], lax.optimization_barrier(jnp.sum(keys_f * keys_f, axis=1)), cosines, sines)
            attended = attend(query_rot, key_rot, value_rows[expert_id, branch_id], key_live)
            projected = jnp.dot(attended, out_weight[expert_id], preferred_element_type=jnp.float32)
            hidden_state = (residual[expert_id, branch_id].astype(jnp.float32) + attn_gate[expert_id][None, :] * projected).astype(jnp.bfloat16)
            branch_hidden.append(hidden_state)
            hidden_f = hidden_state.astype(jnp.float32)
            row_mean = lax.optimization_barrier(jnp.sum(hidden_f, axis=1)) / D
            row_var = lax.optimization_barrier(jnp.sum(hidden_f * hidden_f, axis=1)) / D - row_mean * row_mean
            inv_std = lax.rsqrt(row_var + EPSILON)
            head_in = (hidden_f - row_mean[:, None]) * inv_std[:, None] * (1.0 + head_scale[expert_id])[None, :] + head_shift[expert_id][None, :]
            head_value = jnp.dot(head_in, head_weight[expert_id].astype(jnp.float32), precision=lax.Precision.HIGHEST) + head_bias[expert_id][None, :]
            branch_velocity.append(head_value)
        guide = GUIDE_HIGH if expert_id == 0 else GUIDE_LOW
        guided = branch_velocity[1] + guide * (branch_velocity[0] - branch_velocity[1])
        step_now = step_index[expert_id].astype(jnp.float32)
        delta = noise_level(1.0 - (step_now + 1.0) / STEPS) - noise_level(1.0 - step_now / STEPS)
        hidden_rows.append(jnp.stack(branch_hidden))
        velocities.append(guided)
        advanced_rows.append(latent[expert_id] + delta * guided)
    relayed = jnp.stack([advanced_rows[1], advanced_rows[0]])
    return (jnp.stack(hidden_rows), jnp.stack(velocities), relayed)
```

```python
import math

import jax
import jax.numpy as jnp
from jax import lax
from jax.experimental import pallas as pl
from jax.experimental.pallas import tpu as pltpu
from jax.sharding import PartitionSpec as P

D = 5120
HD = 128
GRID_H = 30
GRID_W = 52
STEPS = 40
TOKENS = 2816
EPSILON = 1e-06
THETA = 10000.0
FLOW_SHIFT = 12.0
GUIDE_HIGH = 4.0
GUIDE_LOW = 3.0
MASKED = -1e30

ROWS = 176
WIDTH = 640
COLS = 160
LOCAL_HEADS = 5
HEAD_Z = (0, 1, 3, 4, 6)
SPLIT = 96
PIECE = 24
PADDED = 8 * PIECE
LIVE_FROM = 1280
MESH = pl.DeviceIdType.MESH
LOG2E = 1.4426950408889634


def add_mod(value, step, size):
    return lax.rem(value + (step % size), size)


def rope_tables(positions):
    half_pairs = HD // 2
    third_pairs = half_pairs // 3
    first_pairs = half_pairs - 2 * third_pairs
    frame_tokens = GRID_H * GRID_W
    frame_idx = (positions // frame_tokens).astype(jnp.float32)
    row_idx = (positions % frame_tokens // GRID_W).astype(jnp.float32)
    col_idx = (positions % GRID_W).astype(jnp.float32)
    lane = jnp.arange(HD, dtype=jnp.int32)
    pair_idx = lane // 2
    in_time = pair_idx < first_pairs
    in_rows = pair_idx < first_pairs + third_pairs
    log_theta = math.log(THETA)
    rate_time = jnp.exp(-log_theta * pair_idx.astype(jnp.float32) / first_pairs)
    rate_rows = jnp.exp(-log_theta * (pair_idx - first_pairs).astype(jnp.float32) / third_pairs)
    rate_cols = jnp.exp(
        -log_theta * (pair_idx - first_pairs - third_pairs).astype(jnp.float32) / third_pairs
    )
    rates = jnp.where(in_time, rate_time, jnp.where(in_rows, rate_rows, rate_cols))
    coords = jnp.where(
        in_time[None, :],
        frame_idx[:, None],
        jnp.where(in_rows[None, :], row_idx[:, None], col_idx[:, None]),
    )
    angles = coords * rates[None, :]
    sign = jnp.where(lane % 2 == 0, -1.0, 1.0)
    return (jnp.cos(angles), jnp.sin(angles) * sign[None, :])


def noise_level(frac):
    return FLOW_SHIFT * frac / (1.0 + (FLOW_SHIFT - 1.0) * frac)


def kernel(
    q_ref, k_ref, v_ref, res_ref, qg_ref, kg_ref, cos_ref, sin_ref, w_ref, gate_ref, scale_ref,
    shift_ref, hw_ref, bias_ref, mask_ref, lat_ref,
    hid_ref, vel_ref, rel_ref,
    sq_pad, msg, msg_in, qr, kr, keys, values, queries, logits, outs, att, wg, pk, pk_in,
    quad, fin, lat_in,
    msg_ss, msg_rs, v_ss, v_rs, k_ss, k_rs, q_ss, q_rs, o_ss, o_rs, ag_ss, ag_rs, wp_ss, wp_rs,
    wz_ss, wz_rs, wx_ss, wx_rs, wf_ss, wf_rs, pk_ss, pk_rs, qd_ss, qd_rs, fa_ss, fa_rs, lt_ss, lt_rs,
):
    e = lax.axis_index("expert")
    b = lax.axis_index("branch")
    s = lax.axis_index("seq")
    y = lax.axis_index("tensor")
    z = lax.div(s, 2)
    x_lo = lax.rem(s, 2)
    x = 2 * b + x_lo

    def remote(src, dst, send_sem, recv_sem, device):
        return pltpu.make_async_remote_copy(
            src_ref=src, dst_ref=dst, send_sem=send_sem, recv_sem=recv_sem,
            device_id=device, device_id_type=MESH,
        )

    def arrived(ref, sem):
        pltpu.make_async_copy(ref, ref, sem).wait()

    def x_device(where):
        return {"branch": lax.div(where, 2), "seq": 2 * z + lax.rem(where, 2)}

    def z_device(where):
        return {"seq": 2 * where + x_lo}

    x_up, x_down = add_mod(x, 1, 4), add_mod(x, -1, 4)
    z_up, z_down = add_mod(z, 1, 8), add_mod(z, -1, 8)
    y_up, y_down = add_mod(y, 1, 8), add_mod(y, -1, 8)

    w_to = {"branch": lax.rem(z, 2), "seq": 2 * y + x_lo, "tensor": 4 * b + lax.div(z, 2)}
    w_from = {
        "branch": lax.div(y, 4),
        "seq": 2 * (2 * lax.rem(y, 4) + b) + x_lo,
        "tensor": z,
    }
    w_stays = jnp.logical_and(
        jnp.logical_and(lax.rem(z, 2) == b, y == z), 4 * b + lax.div(z, 2) == y
    )

    barrier = pltpu.get_barrier_semaphore()

    def greet(device):
        pl.semaphore_signal(barrier, inc=1, device_id=device, device_id_type=MESH)

    for step in range(1, 16):
        greet({"seq": add_mod(s, step, 16)})
    for step in range(1, 8):
        greet({"tensor": add_mod(y, step, 8)})
    greet(x_device(x_up))
    greet(x_device(x_down))
    greet({"branch": 1 - b})
    greet({"expert": 1 - e})
    greet({"expert": 1 - e, "branch": 1 - b})

    @pl.when(jnp.logical_not(w_stays))
    def _():
        greet(w_from)

    def squares(ref):
        total = jnp.zeros((ROWS, HD), jnp.float32)
        for h in range(LOCAL_HEADS):
            part = ref[:, h * HD:(h + 1) * HD].astype(jnp.float32)
            total = total + part * part
        sq_pad[0:ROWS, :] = total
        return jnp.sum(sq_pad[...].T, axis=0, keepdims=True)

    sq_pad[ROWS:, :] = jnp.zeros((256 - ROWS, HD), jnp.float32)
    msg[...] = jnp.zeros_like(msg)
    msg[0:1, :] = squares(q_ref)
    msg[1:2, :] = squares(k_ref)
    weight_f = hw_ref[...].astype(jnp.float32)
    scale_row = 1.0 + scale_ref[...]
    msg[2:3, 0:64] = jnp.dot(scale_row, weight_f, precision=lax.Precision.HIGHEST)
    msg[3:4, 0:64] = jnp.dot(shift_ref[...], weight_f, precision=lax.Precision.HIGHEST)
    pk[ROWS:, :] = jnp.zeros((PADDED - ROWS, HD), jnp.float32)

    pl.semaphore_wait(barrier, 28 - w_stays.astype(jnp.int32))

    msg_copies = [
        remote(msg, msg_in.at[i - 1], msg_ss.at[i - 1], msg_rs.at[i - 1],
               {"tensor": add_mod(y, i, 8)})
        for i in range(1, 8)
    ]
    for copy in msg_copies:
        copy.start()

    my_rows = pl.ds(pl.multiple_of(s * ROWS, 16), ROWS)

    def to_head(src_of, dst, ss, rs):
        copies = []
        for h in range(LOCAL_HEADS):
            for half in range(2):
                target = 2 * HEAD_Z[h] + half
                src, place = src_of(h), dst.at[my_rows, :]
                copies.append((
                    s == target,
                    pltpu.make_async_copy(src, place, rs.at[s]),
                    remote(src, place, ss.at[2 * h + half], rs.at[s], {"seq": target}),
                ))
        return copies

    def start_all(copies):
        for here, local, far in copies:
            pl.when(here)(local.start)
            pl.when(jnp.logical_not(here))(far.start)

    def sent_all(copies):
        for here, local, far in copies:
            pl.when(jnp.logical_not(here))(far.wait_send)

    v_copies = to_head(lambda h: v_ref.at[:, pl.ds(h * HD, HD)], values, v_ss, v_rs)
    k_copies = to_head(lambda h: kr.at[h], keys, k_ss, k_rs)
    q_copies = []
    for h in range(LOCAL_HEADS):
        place = queries.at[z]
        q_copies.append((
            z == HEAD_Z[h],
            pltpu.make_async_copy(qr.at[h], place, q_rs.at[z]),
            remote(qr.at[h], place, q_ss.at[h], q_rs.at[z], z_device(HEAD_Z[h])),
        ))

    start_all(v_copies)
    lat_copy = remote(lat_ref, lat_in, lt_ss, lt_rs, {"expert": 1 - e})
    lat_copy.start()

    def w_slot(at_z, at_x, first=0, count=COLS):
        return wg.at[at_z, pl.ds(pl.multiple_of(at_x * COLS + first, 16), count), :]

    w_place = w_slot(y, 2 * lax.rem(z, 2) + x_lo)
    w_far = remote(w_ref, w_place, wp_ss, wp_rs, w_to)
    w_near = pltpu.make_async_copy(w_ref, w_place, wp_rs)
    pl.when(w_stays)(w_near.start)
    pl.when(jnp.logical_not(w_stays))(w_far.start)

    for i in range(7):
        arrived(msg_in.at[i], msg_rs.at[i])
    sums = msg[...]
    for i in range(7):
        sums = sums + msg_in[i]
    inverse = lax.rsqrt(sums[0:2, :] / D + EPSILON)
    head_u = sums[2:3, 0:64]
    head_c = sums[3:4, 0:64]

    even = lax.rem(lax.broadcasted_iota(jnp.int32, (ROWS, HD), 1), 2) == 0

    def normalize_rotate(ref, gain_ref, row, out):
        column = jnp.broadcast_to(inverse[row:row + 1, :], (HD, 256)).T[0:ROWS, :]
        for h in range(LOCAL_HEADS):
            part = ref[:, h * HD:(h + 1) * HD].astype(jnp.float32)
            part = part * column * gain_ref[:, h * HD:(h + 1) * HD]
            swapped = jnp.where(even, pltpu.roll(part, HD - 1, 1), pltpu.roll(part, 1, 1))
            out[h] = (part * cos_ref[...] + swapped * sin_ref[...]).astype(jnp.bfloat16)

    normalize_rotate(k_ref, kg_ref, 1, kr)
    start_all(k_copies)
    normalize_rotate(q_ref, qg_ref, 0, qr)
    start_all(q_copies)

    half_cols = COLS // 2
    wz_copies = []
    for step in range(1, 5):
        up_slot = add_mod(z, -(step - 1), 8)
        down_slot = add_mod(z, step - 1, 8)
        if step < 4:
            up, down = w_slot(up_slot, x), w_slot(down_slot, x)
        else:
            up = w_slot(up_slot, x, 0, half_cols)
            down = w_slot(down_slot, x, half_cols, half_cols)
        wz_copies.append((
            remote(up, up, wz_ss.at[0, step - 1], wz_rs.at[0, step - 1], z_device(z_up)),
            remote(down, down, wz_ss.at[1, step - 1], wz_rs.at[1, step - 1], z_device(z_down)),
        ))

    def z_slot(j):
        k = (j + 1) // 2
        return add_mod(z, k if j % 2 else -k, 8)

    wx_copies, wf_copies = [], []
    for j in range(8):
        at_z = z_slot(j)
        own = w_slot(at_z, x)
        wx_copies.append((
            remote(own, own, wx_ss.at[j, 0], wx_rs.at[j, 0], x_device(x_up)),
            remote(own, own, wx_ss.at[j, 1], wx_rs.at[j, 1], x_device(x_down)),
        ))
        first = w_slot(at_z, x_down, 0, half_cols)
        second = w_slot(at_z, x_up, half_cols, half_cols)
        wf_copies.append((
            remote(first, first, wf_ss.at[j, 0], wf_rs.at[j, 0], x_device(x_up)),
            remote(second, second, wf_ss.at[j, 1], wf_rs.at[j, 1], x_device(x_down)),
        ))

    def w_event(j):
        if j == 0:
            arrived(w_slot(z, x), wp_rs)
            wz_copies[0][0].start()
            wz_copies[0][1].start()
        elif j < 7:
            k = (j + 1) // 2
            way = j % 2
            arrived(w_slot(z_slot(j), x), wz_rs.at[way, k - 1])
            if k < 4:
                wz_copies[k][way].start()
        elif j == 7:
            arrived(w_slot(z_slot(7), x, 0, half_cols), wz_rs.at[0, 3])
            arrived(w_slot(z_slot(7), x, half_cols, half_cols), wz_rs.at[1, 3])
        if j < 8:
            wx_copies[j][0].start()
            wx_copies[j][1].start()
        if j > 0:
            at_z = z_slot(j - 1)
            arrived(w_slot(at_z, x_down), wx_rs.at[j - 1, 0])
            wf_copies[j - 1][0].start()
            arrived(w_slot(at_z, x_up), wx_rs.at[j - 1, 1])
            wf_copies[j - 1][1].start()

    w_event(0)
    w_event(1)
    w_event(2)

    attends = z == HEAD_Z[0]
    head = jnp.int32(0)
    for h in range(1, LOCAL_HEADS):
        attends = jnp.logical_or(attends, z == HEAD_Z[h])
        head = head + (z >= HEAD_Z[h]).astype(jnp.int32)
    head_cols = pl.ds(pl.multiple_of(head * HD, HD), HD)
    att_place = att.at[y, :, head_cols]

    @pl.when(attends)
    def _():
        for i in range(8):
            arrived(queries.at[i], q_rs.at[i])
        for i in range(16):
            arrived(keys.at[pl.ds(i * ROWS, ROWS), :], k_rs.at[i])
        for i in range(16):
            arrived(values.at[pl.ds(i * ROWS, ROWS), :], v_rs.at[i])

    def o_far(j):
        return remote(outs.at[j], att_place, o_ss.at[j], o_rs.at[head], z_device(j))

    factor = HD ** -0.5 * LOG2E

    def attend(j):
        query = queries[j]
        peak = None
        for c in range(TOKENS // 256):
            cols = slice(c * 256, (c + 1) * 256)
            part = lax.dot_general(
                query, keys[cols, :], (((1,), (1,)), ((), ())),
                preferred_element_type=jnp.float32,
            )
            if c * 256 >= LIVE_FROM:
                part = part + mask_ref[:, cols]
            logits[:, cols] = part
            top = jnp.maximum(part[:, 0:HD], part[:, HD:])
            peak = top if peak is None else jnp.maximum(peak, top)
        peak = jnp.max(peak, axis=1, keepdims=True)
        total = jnp.zeros((ROWS, HD), jnp.float32)
        mixed = jnp.zeros((ROWS, HD), jnp.float32)
        for c in range(TOKENS // 256):
            cols = slice(c * 256, (c + 1) * 256)
            prob = jnp.exp2((logits[:, cols] - peak) * factor)
            total = total + (prob[:, 0:HD] + prob[:, HD:])
            mixed = mixed + jnp.dot(
                prob.astype(jnp.bfloat16), values[cols, :], preferred_element_type=jnp.float32
            )
        denom = jnp.sum(total, axis=1, keepdims=True)
        outs[j] = (mixed / denom).astype(jnp.bfloat16)

    def one_block(j, carry):
        @pl.when(attends)
        def _():
            attend(j)
            pl.when(j == z)(
                pltpu.make_async_copy(outs.at[j], att_place, o_rs.at[head]).start
            )
            pl.when(j != z)(o_far(j).start)

        for turn, event in ((2, 3), (5, 4)):
            @pl.when(j == turn)
            def _():
                w_event(event)
        return carry

    lax.fori_loop(0, 8, one_block, 0)

    ag_copies = []
    for step in range(1, 5):
        up_block = att.at[add_mod(y, -(step - 1), 8)]
        down_block = att.at[add_mod(y, step - 1, 8)]
        if step == 4:
            up_block = up_block.at[pl.ds(0, SPLIT), :]
            down_block = down_block.at[pl.ds(SPLIT, ROWS - SPLIT), :]
        ag_copies.append((
            remote(up_block, up_block, ag_ss.at[0, step - 1], ag_rs.at[0, step - 1],
                   {"tensor": y_up}),
            remote(down_block, down_block, ag_ss.at[1, step - 1], ag_rs.at[1, step - 1],
                   {"tensor": y_down}),
        ))

    for h in range(LOCAL_HEADS):
        arrived(att.at[y, :, pl.ds(h * HD, HD)], o_rs.at[h])
    for step in range(1, 5):
        ag_copies[step - 1][0].start()
        ag_copies[step - 1][1].start()
        if step < 4:
            w_event(4 + step)
            arrived(att.at[add_mod(y, -step, 8)], ag_rs.at[0, step - 1])
            arrived(att.at[add_mod(y, step, 8)], ag_rs.at[1, step - 1])
    w_event(8)
    across = att.at[add_mod(y, 4, 8)]
    arrived(across.at[pl.ds(0, SPLIT), :], ag_rs.at[0, 3])
    arrived(across.at[pl.ds(SPLIT, ROWS - SPLIT), :], ag_rs.at[1, 3])
    for j in range(8):
        at_z = z_slot(j)
        arrived(w_slot(at_z, add_mod(x, 2, 4), 0, half_cols), wf_rs.at[j, 0])
        arrived(w_slot(at_z, add_mod(x, 2, 4), half_cols, half_cols), wf_rs.at[j, 1])

    projected = jnp.zeros((ROWS, WIDTH), jnp.float32)
    for t in range(8):
        projected = projected + lax.dot_general(
            att[t], wg[t], (((1,), (1,)), ((), ())), preferred_element_type=jnp.float32
        )
    hidden = (res_ref[...].astype(jnp.float32) + gate_ref[...] * projected).astype(jnp.bfloat16)
    hid_ref[...] = hidden
    hidden_f = hidden.astype(jnp.float32)
    pk[0:ROWS, 0:64] = jnp.dot(
        hidden_f * scale_row, weight_f, precision=lax.Precision.HIGHEST
    )
    lane = lax.broadcasted_iota(jnp.int32, (ROWS, 64), 1)
    row_sum = jnp.sum(hidden_f, axis=1, keepdims=True)
    row_sq = jnp.sum(hidden_f * hidden_f, axis=1, keepdims=True)
    pk[0:ROWS, 64:128] = jnp.where(lane == 0, row_sum, jnp.where(lane == 1, row_sq, 0.0))

    def piece(ref, at):
        return ref.at[pl.ds(pl.multiple_of(at * PIECE, 8), PIECE), :]

    pk_copies = [
        remote(piece(pk, add_mod(y, i, 8)), pk_in.at[i - 1], pk_ss.at[i - 1], pk_rs.at[i - 1],
               {"tensor": add_mod(y, i, 8)})
        for i in range(1, 8)
    ]
    for copy in pk_copies:
        copy.start()
    my_piece = pl.ds(pl.multiple_of(y * PIECE, 8), PIECE)
    total = pk[my_piece, :]
    for i in range(7):
        arrived(pk_in.at[i], pk_rs.at[i])
    for i in range(7):
        total = total + pk_in[i]
    mean = total[:, 64:65] / D
    inv_std = lax.rsqrt(total[:, 65:66] / D - mean * mean + EPSILON)
    value = inv_std * (total[:, 0:64] - mean * head_u) + head_c + bias_ref[...]
    slot = 2 * e + b
    quad[slot, :, 0:64] = value
    quad[slot, :, 64:128] = value
    qd_copies = [
        remote(quad.at[slot], quad.at[slot], qd_ss.at[i], qd_rs.at[i], device)
        for i, device in enumerate((
            {"branch": 1 - b}, {"expert": 1 - e}, {"expert": 1 - e, "branch": 1 - b},
        ))
    ]
    for copy in qd_copies:
        copy.start()
    arrived(lat_in, lt_rs)
    arrived(quad.at[2 * e + (1 - b)], qd_rs.at[0])
    arrived(quad.at[2 * (1 - e) + b], qd_rs.at[1])
    arrived(quad.at[2 * (1 - e) + (1 - b)], qd_rs.at[2])

    def guided(expert):
        guide = jnp.where(expert == 0, GUIDE_HIGH, GUIDE_LOW)
        cond, uncond = quad[2 * expert], quad[2 * expert + 1]
        return uncond + guide * (cond - uncond)

    latent = lat_in[my_piece, :]
    fin[my_piece, 0:64] = guided(e)[:, 0:64]
    fin[my_piece, 64:128] = latent[:, 0:64] + latent[:, 64:128] * guided(1 - e)[:, 0:64]
    fa_copies = [
        remote(piece(fin, y), piece(fin, y), fa_ss.at[i - 1], fa_rs.at[i - 1],
               {"tensor": add_mod(y, i, 8)})
        for i in range(1, 8)
    ]
    for copy in fa_copies:
        copy.start()
    for i in range(1, 8):
        arrived(piece(fin, add_mod(y, -i, 8)), fa_rs.at[i - 1])
    vel_ref[...] = fin[0:ROWS, 0:64]
    rel_ref[...] = fin[0:ROWS, 64:128]

    for copy in msg_copies + pk_copies + qd_copies + fa_copies + [lat_copy]:
        copy.wait_send()
    sent_all(v_copies + k_copies + q_copies)
    pl.when(jnp.logical_not(w_stays))(w_far.wait_send)
    for up, down in wz_copies + wx_copies + wf_copies + ag_copies:
        up.wait_send()
        down.wait_send()

    @pl.when(attends)
    def _():
        for j in range(8):
            pl.when(z != j)(o_far(j).wait_send)


def local(
    query_raw,
    key_raw,
    value_rows,
    residual,
    latent,
    query_gain,
    key_gain,
    out_weight,
    attn_gate,
    head_shift,
    head_scale,
    head_weight,
    head_bias,
    valid_rows,
    step_index,
):
    seq_id = lax.axis_index("seq")
    positions = seq_id * ROWS + jnp.arange(ROWS, dtype=jnp.int32)
    cosines, sines = rope_tables(positions)
    key_live = jnp.arange(TOKENS, dtype=jnp.int32) < valid_rows[0] * GRID_W
    mask = jnp.where(key_live, 0.0, MASKED)[None, :].astype(jnp.float32)
    step_now = step_index[0].astype(jnp.float32)
    delta = noise_level(1.0 - (step_now + 1.0) / STEPS) - noise_level(1.0 - step_now / STEPS)
    latent_delta = jnp.pad(
        jnp.concatenate([latent[0], jnp.broadcast_to(delta, latent[0].shape)], axis=1),
        ((0, PADDED - ROWS), (0, 0)),
    )
    vmem = pl.BlockSpec(memory_space=pltpu.VMEM)
    dma = pltpu.SemaphoreType.DMA
    f32, bf16 = jnp.float32, jnp.bfloat16
    hidden, velocity, relayed = pl.pallas_call(
        kernel,
        out_shape=(
            jax.ShapeDtypeStruct((ROWS, WIDTH), bf16),
            jax.ShapeDtypeStruct((ROWS, 64), f32),
            jax.ShapeDtypeStruct((ROWS, 64), f32),
        ),
        in_specs=[vmem] * 16,
        out_specs=(vmem, vmem, vmem),
        scratch_shapes=[
            pltpu.VMEM((256, HD), f32),
            pltpu.VMEM((8, 256), f32),
            pltpu.VMEM((7, 8, 256), f32),
            pltpu.VMEM((LOCAL_HEADS, ROWS, HD), bf16),
            pltpu.VMEM((LOCAL_HEADS, ROWS, HD), bf16),
            pltpu.VMEM((TOKENS, HD), bf16),
            pltpu.VMEM((TOKENS, HD), bf16),
            pltpu.VMEM((8, ROWS, HD), bf16),
            pltpu.VMEM((ROWS, TOKENS), f32),
            pltpu.VMEM((8, ROWS, HD), bf16),
            pltpu.VMEM((8, ROWS, WIDTH), bf16),
            pltpu.VMEM((8, WIDTH, WIDTH), bf16),
            pltpu.VMEM((PADDED, HD), f32),
            pltpu.VMEM((7, PIECE, HD), f32),
            pltpu.VMEM((4, PIECE, HD), f32),
            pltpu.VMEM((PADDED, HD), f32),
            pltpu.VMEM((PADDED, HD), f32),
            dma((7,)), dma((7,)),
            dma((10,)), dma((16,)),
            dma((10,)), dma((16,)),
            dma((5,)), dma((8,)),
            dma((8,)), dma((5,)),
            dma((2, 4)), dma((2, 4)),
            dma, dma,
            dma((2, 4)), dma((2, 4)),
            dma((8, 2)), dma((8, 2)),
            dma((8, 2)), dma((8, 2)),
            dma((7,)), dma((7,)),
            dma((3,)), dma((3,)),
            dma((7,)), dma((7,)),
            dma, dma,
        ],
        compiler_params=pltpu.CompilerParams(
            collective_id=0, has_side_effects=True, vmem_limit_bytes=56 * 1024 * 1024
        ),
    )(
        query_raw[0, 0], key_raw[0, 0], value_rows[0, 0], residual[0, 0], query_gain, key_gain,
        cosines, sines, out_weight[0].T, attn_gate, head_scale, head_shift, head_weight[0],
        head_bias, mask, latent_delta,
    )
    return (hidden[None, None], velocity[None], relayed[None])


def solution(mesh):
    placed = (
        P("expert", "branch", "seq", "tensor"),
        P("expert", "branch", "seq", "tensor"),
        P("expert", "branch", "seq", "tensor"),
        P("expert", "branch", "seq", "tensor"),
        P("expert", "seq", None),
        P("expert", "tensor"),
        P("expert", "tensor"),
        P("expert", "tensor", ("branch", "seq")),
        P("expert", "tensor"),
        P("expert", "tensor"),
        P("expert", "tensor"),
        P("expert", "tensor", None),
        P("expert", None),
        P("expert"),
        P("expert"),
    )
    return jax.shard_map(
        local,
        mesh=mesh,
        in_specs=placed,
        out_specs=(
            P("expert", "branch", "seq", "tensor"),
            P("expert", "seq", None),
            P("expert", "seq", None),
        ),
        check_vma=False,
    )
```

```python
import math

import jax
import jax.numpy as jnp
from jax import lax
from jax.experimental import pallas as pl
from jax.experimental.pallas import tpu as pltpu
from jax.sharding import PartitionSpec as P

D = 5120
HD = 128
GRID_H = 30
GRID_W = 52
STEPS = 40
TOKENS = 2816
EPSILON = 1e-06
THETA = 10000.0
FLOW_SHIFT = 12.0
GUIDE_HIGH = 4.0
GUIDE_LOW = 3.0
MASKED = -1e30

ROWS = 176
WIDTH = 640
COLS = 160
LOCAL_HEADS = 5
HEAD_Z = (0, 1, 3, 4, 6)
UPPER = 96
W_COPIES = 31
LIVE_FROM = 1280
MESH = pl.DeviceIdType.MESH
LOG2E = 1.4426950408889634


def add_mod(value, step, size):
    return lax.rem(value + (step % size), size)


def rope_tables(first_position):
    half_pairs = HD // 2
    third_pairs = half_pairs // 3
    first_pairs = half_pairs - 2 * third_pairs
    frame_tokens = GRID_H * GRID_W
    position = first_position + lax.broadcasted_iota(jnp.int32, (ROWS, HD), 0)
    frame = (position >= frame_tokens).astype(jnp.int32)
    for later in range(2, (TOKENS - 1) // frame_tokens + 1):
        frame = frame + (position >= later * frame_tokens).astype(jnp.int32)
    inside = (position - frame * frame_tokens).astype(jnp.float32)
    row = jnp.floor((inside + 0.5) * (1.0 / GRID_W))
    col = inside - row * GRID_W
    lane = lax.broadcasted_iota(jnp.int32, (ROWS, HD), 1)
    pair = lax.shift_right_logical(lane, 1)
    in_time = pair < first_pairs
    in_rows = pair < first_pairs + third_pairs
    offset = jnp.where(in_time, 0, jnp.where(in_rows, first_pairs, first_pairs + third_pairs))
    count = jnp.where(in_time, float(first_pairs), float(third_pairs))
    rates = jnp.exp(-math.log(THETA) * (pair - offset).astype(jnp.float32) / count)
    coords = jnp.where(in_time, frame.astype(jnp.float32), jnp.where(in_rows, row, col))
    angles = coords * rates
    odd = jnp.bitwise_and(lane, 1) == 1
    sines = jnp.sin(angles)
    return jnp.cos(angles), jnp.where(odd, sines, -sines), odd


def noise_level(frac):
    return FLOW_SHIFT * frac / (1.0 + (FLOW_SHIFT - 1.0) * frac)


def kernel(
    q_ref, k_ref, v_ref, res_ref, qg_ref, kg_ref, w_ref, gate_ref, scale_ref,
    shift_ref, hw_ref, bias_ref, lat_ref, valid_ref, step_ref,
    hid_ref, vel_ref, rel_ref,
    sq_pad, msg, msg_in, cos, sin, qr, kr, keys, values, queries, mask, logits, outs, att, w_mid, wg, total, px, px_in,
    head_w, bias_row, lat, pk, pk_in, swap, swap_in, fin,
    msg_ss, msg_rs, v_ss, v_rs, k_ss, k_rs, q_ss, q_rs, vr_ss, vr_rs, kr_ss, kr_rs, o_ss, o_rs,
    ag_ss, ag_rs, wm_ss, wm_rs, wp_ss, wp_rs, w_ss, w_rs, px_ss, px_rs, pk_ss, pk_rs, sw_ss, sw_rs,
    fin_ss, fin_rs,
):
    e = lax.axis_index("expert")
    b = lax.axis_index("branch")
    s = lax.axis_index("seq")
    y = lax.axis_index("tensor")
    z = lax.div(s, 2)
    x_lo = lax.rem(s, 2)
    share = 2 * y + b

    def remote(src, dst, send_sem, recv_sem, device):
        return pltpu.make_async_remote_copy(
            src_ref=src, dst_ref=dst, send_sem=send_sem, recv_sem=recv_sem,
            device_id=device, device_id_type=MESH,
        )

    def arrived(ref, sem):
        pltpu.make_async_copy(ref, ref, sem).wait()

    def z_device(where):
        return {"seq": 2 * where + x_lo}

    def share_device(where):
        return {"branch": lax.rem(where, 2), "tensor": lax.div(where, 2)}

    z_up, z_down = add_mod(z, 1, 8), add_mod(z, -1, 8)
    y_up, y_down = add_mod(y, 1, 8), add_mod(y, -1, 8)
    beside = {"seq": s + 1 - 2 * x_lo}

    across = {"branch": 1 - b, "seq": 2 * z + 1 - x_lo}
    holds = lax.rem(y + b, 2) == 0
    off = lax.rem(y + b, 2)

    mid_z = 2 * lax.rem(lax.div(y, 2) + 4 - lax.div(z, 2), 4) + lax.rem(z, 2)
    to_y = 4 * b + lax.div(mid_z, 2)
    w_turns = lax.rem(y, 2) != b
    w_to = {
        "branch": lax.rem(y, 2),
        "seq": 2 * z + jnp.where(w_turns, 1 - x_lo, x_lo),
        "tensor": to_y,
    }
    turned = lax.div(y, 4) != b
    w_from = {
        "branch": lax.div(y, 4),
        "seq": 2 * z + jnp.where(turned, 1 - x_lo, x_lo),
        "tensor": 2 * lax.rem(lax.div(z, 2) + y, 4) + b,
    }
    w_stays_mid = mid_z == z
    w_stays = jnp.logical_and(lax.rem(y, 2) == b, to_y == y)

    barrier = pltpu.get_barrier_semaphore()

    def greet(device):
        pl.semaphore_signal(barrier, inc=1, device_id=device, device_id_type=MESH)

    for step in range(1, 8):
        greet(z_device(add_mod(z, step, 8)))
    for step in range(8):
        greet({"branch": 1 - b, "seq": 2 * add_mod(z, step, 8) + 1 - x_lo})
    for step in range(1, 16):
        greet(share_device(add_mod(share, step, 16)))
    greet(beside)
    greet({"expert": 1 - e})
    pl.when(jnp.logical_not(w_stays))(lambda: greet(w_from))

    def squares(ref):
        summed = jnp.zeros((ROWS, HD), jnp.float32)
        for h in range(LOCAL_HEADS):
            part = ref[:, h * HD:(h + 1) * HD].astype(jnp.float32)
            summed = summed + part * part
        sq_pad[0:ROWS, :] = summed
        return jnp.sum(sq_pad[...].T, axis=0, keepdims=True)

    sq_pad[ROWS:, :] = jnp.zeros((256 - ROWS, HD), jnp.float32)
    msg[...] = jnp.zeros_like(msg)
    for at, ref in enumerate((q_ref, k_ref)):
        row = squares(ref)
        msg[2 * at:2 * at + 1, :] = row[:, 0:HD]
        msg[2 * at + 1:2 * at + 2, :] = row[:, HD:]

    pl.semaphore_wait(barrier, 33 - w_stays.astype(jnp.int32))

    w_mid_far = remote(w_ref, w_mid, wm_ss, wm_rs, z_device(mid_z))
    w_mid_near = pltpu.make_async_copy(w_ref, w_mid, wm_rs)
    pl.when(w_stays_mid)(w_mid_near.start)
    pl.when(jnp.logical_not(w_stays_mid))(w_mid_far.start)

    msg_copies = [
        remote(msg, msg_in.at[i - 1], msg_ss.at[i - 1], msg_rs.at[i - 1],
               {"tensor": add_mod(y, i, 8)})
        for i in range(1, 8)
    ]
    for copy in msg_copies:
        copy.start()

    my_rows = pl.ds(pl.multiple_of(s * ROWS, 16), ROWS)

    def to_head(src_of, place, ss, rs):
        copies = []
        for h in range(LOCAL_HEADS):
            copies.append((
                z == HEAD_Z[h],
                pltpu.make_async_copy(src_of(h), place, rs.at[z]),
                remote(src_of(h), place, ss.at[h], rs.at[z], z_device(HEAD_Z[h])),
            ))
        return copies

    def start_all(copies):
        for here, local_copy, far in copies:
            pl.when(here)(local_copy.start)
            pl.when(jnp.logical_not(here))(far.start)

    def sent_all(copies):
        for here, _, far in copies:
            pl.when(jnp.logical_not(here))(far.wait_send)

    v_copies = to_head(lambda h: v_ref.at[:, pl.ds(h * HD, HD)], values.at[my_rows, :], v_ss, v_rs)
    k_copies = to_head(lambda h: kr.at[h], keys.at[my_rows, :], k_ss, k_rs)
    q_copies = to_head(lambda h: qr.at[h], queries.at[z], q_ss, q_rs)
    start_all(v_copies)

    cos_table, sin_table, odd = rope_tables(s * ROWS)
    cos[...] = cos_table
    sin[...] = sin_table
    limit = valid_ref[0] * GRID_W
    key_at = lax.broadcasted_iota(jnp.int32, (1, TOKENS), 1)
    mask[...] = jnp.where(key_at < limit, 0.0, MASKED)
    bias_row[...] = jnp.zeros_like(bias_row)
    bias_row[:, 0:64] = bias_ref[...]
    bias_col = jnp.broadcast_to(bias_row[...], (HD, HD)).T[0:64, 0:1]
    weight_f = hw_ref[...].astype(jnp.float32)
    scaled = weight_f * (1.0 + scale_ref[...])
    head_u = jnp.sum(scaled, axis=1, keepdims=True)
    head_c = jnp.sum(weight_f * shift_ref[...], axis=1, keepdims=True)
    head_c = head_c + jnp.where(y == 0, bias_col, 0.0)
    lane = lax.broadcasted_iota(jnp.int32, (64, HD), 1)
    extra = jnp.where(lane == ROWS - HD, head_u, jnp.where(lane == ROWS - HD + 1, head_c, 0.0))
    head_w[...] = jnp.zeros_like(head_w)
    pk[...] = jnp.zeros_like(pk)
    swap[...] = jnp.zeros_like(swap)
    fin[...] = jnp.zeros_like(fin)
    for i in range(16):
        head_w[8 * i:8 * i + 4, :] = scaled[4 * i:4 * i + 4, :]
        head_w[8 * i + 4:8 * i + 5, :] = jnp.ones((1, WIDTH), jnp.float32)
        pk[i, 0:4, HD:] = extra[4 * i:4 * i + 4, :]
        lat[i, 0:4, :] = lat_ref[4 * i:4 * i + 4, :]

    for i in range(7):
        arrived(msg_in.at[i], msg_rs.at[i])
    sums = msg[...]
    for i in range(7):
        sums = sums + msg_in[i]
    inverse = lax.rsqrt(sums / D + EPSILON)

    def normalize_rotate(ref, gain_ref, first, out):
        column = jnp.concatenate(
            [
                jnp.broadcast_to(inverse[first:first + 1, :], (HD, HD)).T,
                jnp.broadcast_to(inverse[first + 1:first + 2, :], (HD, HD)).T[0:ROWS - HD, :],
            ],
            axis=0,
        )
        for h in range(LOCAL_HEADS):
            part = ref[:, h * HD:(h + 1) * HD].astype(jnp.float32)
            part = part * column * gain_ref[:, h * HD:(h + 1) * HD]
            swapped = jnp.where(odd, pltpu.roll(part, 1, 1), pltpu.roll(part, HD - 1, 1))
            out[h] = (part * cos[...] + swapped * sin[...]).astype(jnp.bfloat16)

    normalize_rotate(k_ref, kg_ref, 2, kr)
    start_all(k_copies)
    normalize_rotate(q_ref, qg_ref, 0, qr)
    start_all(q_copies)

    slots = {}
    base_x = jnp.where(turned, 1 - x_lo, x_lo)
    for dz in range(8):
        at_z = add_mod(z, dz, 8)
        at = lax.rem(lax.div(at_z, 2) + y, 4)
        for dx in range(2):
            at_x = 1 - base_x if dx else base_x
            slots[dz, dx] = (at, (2 * lax.rem(at_z, 2) + at_x) * COLS)

    def w_slot(dz, dx, first=0, count=COLS):
        at, row = slots[dz % 8, dx]
        return wg.at[at, pl.ds(pl.multiple_of(row + first, 16), count), :]

    def upper(dz, dx):
        return w_slot(dz, dx, 0, UPPER)

    def lower(dz, dx):
        return w_slot(dz, dx, UPPER, COLS - UPPER)

    def upper_half(dz, way):
        return w_slot(dz, 0, way * (UPPER // 2), UPPER // 2)

    w_sent, w_index = {}, {}

    def w_copy(key, block, device):
        at = w_index.setdefault(key, len(w_index))
        w_sent[key] = remote(block, block, w_ss.at[at], w_rs.at[at], device)

    def w_wait(key, block):
        arrived(block, w_rs.at[w_index[key]])

    z_to = (z_device(z_up), z_device(z_down))

    def ring_slot(j):
        k = (j + 1) // 2
        return k if j % 2 else -k

    for way in range(2):
        sign = 1 if way else -1
        for k in range(1, 5):
            held = sign * (k - 1)
            w_copy(("z", k, way), upper(held, 0) if k < 4 else upper_half(held, way), z_to[way])
            for dx in range(2):
                if k < 4 or dx == way:
                    w_copy(("lz", k, way, dx), lower(held, dx), z_to[way])
    w_copy("lx", lower(0, 0), beside)
    for j in range(8):
        w_copy(("ux", j), upper(ring_slot(j), 0), beside)

    w_near = pltpu.make_async_copy(w_mid, w_slot(0, 0), wp_rs)
    to_row = (2 * lax.rem(z, 2) + x_lo) * COLS
    w_far = remote(
        w_mid, wg.at[lax.div(y, 2), pl.ds(pl.multiple_of(to_row, 16), COLS), :], wp_ss, wp_rs,
        w_to,
    )

    def w_event(name):
        if name == "along y":
            arrived(w_mid, wm_rs)
            pl.when(w_stays)(w_near.start)
            pl.when(jnp.logical_not(w_stays))(w_far.start)
        elif name == "start":
            arrived(w_slot(0, 0), wp_rs)
            w_sent["lx"].start()
            for way in range(2):
                w_sent["z", 1, way].start()
            for way in range(2):
                w_sent["lz", 1, way, 0].start()
            w_sent["ux", 0].start()
        elif name == "lower":
            w_wait("lx", lower(0, 1))
            for way in range(2):
                w_sent["lz", 1, way, 1].start()
        elif name == "end":
            for way in range(2):
                w_wait(("z", 4, way), upper_half(4, way))
            w_sent["ux", 7].start()
        elif name == "finish":
            for dx in range(2):
                w_wait(("lz", 4, dx, dx), lower(4, dx))
            for j in range(8):
                w_wait(("ux", j), upper(ring_slot(j), 1))
        else:
            k = name
            for way in (1, 0):
                held = k if way else -k
                w_wait(("z", k, way), upper(held, 0))
                w_sent["z", k + 1, way].start()
                w_sent["ux", 2 * k - way].start()
            for dx in range(2):
                for way in (1, 0):
                    w_wait(("lz", k, way, dx), lower(k if way else -k, dx))
                    if k < 3 or dx == way:
                        w_sent["lz", k + 1, way, dx].start()

    attends = z == HEAD_Z[0]
    head = jnp.int32(0)
    for h in range(1, LOCAL_HEADS):
        attends = jnp.logical_or(attends, z == HEAD_Z[h])
        head = head + (z >= HEAD_Z[h]).astype(jnp.int32)
    head_cols = pl.ds(pl.multiple_of(head * HD, HD), HD)
    att_place = att.at[lax.div(y, 2), b, :, head_cols]

    def block_rows(buf, at_z, at_x):
        return buf.at[pl.ds(pl.multiple_of((2 * at_z + at_x) * ROWS, 16), ROWS), :]

    def relay(buf, at_z, ss, rs):
        block = block_rows(buf, at_z, x_lo)
        return remote(block, block, ss.at[at_z], rs.at[at_z], beside)

    def pass_on(buf, came, ss, rs):
        @pl.when(attends)
        def _():
            def one(i, carry):
                arrived(block_rows(buf, i, x_lo), came.at[i])
                relay(buf, i, ss, rs).start()
                return carry

            lax.fori_loop(0, 8, one, 0)

    pass_on(values, v_rs, vr_ss, vr_rs)
    w_event('along y')
    pass_on(keys, k_rs, kr_ss, kr_rs)

    @pl.when(attends)
    def _():
        def one(i, carry):
            arrived(queries.at[i], q_rs.at[i])
            arrived(block_rows(keys, i, 1 - x_lo), kr_rs.at[i])
            arrived(block_rows(values, i, 1 - x_lo), vr_rs.at[i])
            return carry

        lax.fori_loop(0, 8, one, 0)

    def o_far(at_z):
        return remote(
            outs.at[at_z], att_place, o_ss.at[at_z], o_rs.at[b, head],
            {"branch": lax.rem(y, 2), "seq": 2 * at_z + jnp.where(holds, x_lo, 1 - x_lo)},
        )

    factor = HD ** -0.5 * LOG2E

    def attend(at_z):
        query = queries[at_z]
        peak = None
        for c in range(TOKENS // 256):
            cols = slice(c * 256, (c + 1) * 256)
            part = lax.dot_general(
                query, keys[cols, :], (((1,), (1,)), ((), ())),
                preferred_element_type=jnp.float32,
            )
            if c * 256 >= LIVE_FROM:
                part = part + mask[:, cols]
            logits[:, cols] = part
            top = jnp.maximum(part[:, 0:HD], part[:, HD:])
            peak = top if peak is None else jnp.maximum(peak, top)
        peak = jnp.max(peak, axis=1, keepdims=True)
        summed = jnp.zeros((ROWS, HD), jnp.float32)
        mixed = jnp.zeros((ROWS, HD), jnp.float32)
        for c in range(TOKENS // 256):
            cols = slice(c * 256, (c + 1) * 256)
            prob = jnp.exp2((logits[:, cols] - peak) * factor)
            summed = summed + (prob[:, 0:HD] + prob[:, HD:])
            mixed = mixed + jnp.dot(
                prob.astype(jnp.bfloat16), values[cols, :], preferred_element_type=jnp.float32
            )
        denom = jnp.sum(summed, axis=1, keepdims=True)
        outs[at_z] = (mixed / denom).astype(jnp.bfloat16)

    def one_block(j, carry):
        away = lax.div(8 - j, 2)
        at_z = lax.rem(z + jnp.where(lax.rem(j, 2) == 1, away, 8 - away), 8)

        @pl.when(attends)
        def _():
            attend(at_z)
            stays = jnp.logical_and(at_z == z, holds)
            pl.when(stays)(pltpu.make_async_copy(outs.at[at_z], att_place, o_rs.at[b, head]).start)
            pl.when(jnp.logical_not(stays))(o_far(at_z).start)

        for turn, event in ((0, 'start'), (2, 'lower'), (5, 1)):
            pl.when(j == turn)(lambda: w_event(event))
        return carry

    lax.fori_loop(0, 8, one_block, 0)

    def ag_block(way, away, token_branch, h):
        at_y = lax.rem(y + (away if way else 8 - away), 8)
        return att.at[lax.div(at_y, 2), token_branch, :, pl.ds(h * HD, HD)]

    def ag_last(way, h):
        return h >= 3 if way else h < 3

    ag_starts, ag_lasts = [], []
    for which in range(2):
        for h in range(LOCAL_HEADS):
            at = LOCAL_HEADS * which + h
            tb = b if which else 1 - b
            for way in range(2):
                device = {"tensor": y_down if way else y_up}
                near = ag_block(way, off, tb, h)
                ag_starts.append((which, h, way, remote(
                    near, near, ag_ss.at[way, 0, at], ag_rs.at[way, 0, at], device)))
                far = ag_block(way, off + 2, tb, h)
                ag_lasts.append((which, h, way, remote(
                    far, far, ag_ss.at[way, 1, at], ag_rs.at[way, 1, at], device)))

    def ag_start(which):
        for part, h, way, copy in ag_starts:
            if part != which:
                continue
            at = LOCAL_HEADS * which + h
            tb = b if which else 1 - b
            if way == 0:
                place = att.at[lax.div(y, 2), tb, :, pl.ds(h * HD, HD)]
                pl.when(holds)(lambda: arrived(place, o_rs.at[tb, h]))
            near = ag_block(way, off, tb, h)
            pl.when(jnp.logical_not(holds))(lambda: arrived(near, ag_rs.at[way, 0, at]))
            copy.start()

    def ag_go_on(which):
        for part, h, way, copy in ag_lasts:
            if part != which:
                continue
            at = LOCAL_HEADS * which + h
            arrived(ag_block(way, off + 2, b if which else 1 - b, h), ag_rs.at[way, off, at])
            if ag_last(way, h):
                copy.start()
            else:
                pl.when(holds)(copy.start)

    def ag_finish(which):
        @pl.when(holds)
        def _():
            for h in range(LOCAL_HEADS):
                way = 0 if ag_last(0, h) else 1
                opposite = ag_block(way, 4, b if which else 1 - b, h)
                arrived(opposite, ag_rs.at[way, 1, LOCAL_HEADS * which + h])

    def project(tb):
        def one_group(g, carry):
            part = lax.dot_general(
                att[g, tb], wg[g], (((1,), (1,)), ((), ())), preferred_element_type=jnp.float32
            )
            total[...] += part
            return carry

        total[...] = jnp.zeros_like(total)
        lax.fori_loop(0, 4, one_group, 0)
        return total[...]

    ag_start(0)
    w_event(2)
    ag_start(1)
    w_event(3)
    ag_go_on(0)
    w_event('end')
    ag_go_on(1)
    ag_finish(0)
    w_event('finish')
    px[...] = project(1 - b).astype(jnp.bfloat16)
    px_copy = remote(px, px_in, px_ss, px_rs, across)
    px_copy.start()
    ag_finish(1)
    projected = project(b)
    arrived(px_in, px_rs)
    projected = projected + px_in[...].astype(jnp.float32)
    hidden = (res_ref[...].astype(jnp.float32) + gate_ref[...] * projected).astype(jnp.bfloat16)
    hid_ref[...] = hidden
    hidden_f = hidden.astype(jnp.float32)

    over_features = (((1,), (1,)), ((), ()))
    sums = lax.dot_general(
        head_w[...], hidden_f, over_features, precision=lax.Precision.HIGHEST,
        preferred_element_type=jnp.float32,
    ).reshape(16, 8, ROWS)
    square_sums = lax.dot_general(
        jnp.ones((8, WIDTH), jnp.float32), hidden_f * hidden_f, over_features,
        precision=lax.Precision.HIGHEST, preferred_element_type=jnp.float32,
    )
    sixth = lax.broadcasted_iota(jnp.int32, (16, 8, ROWS), 1) == 5
    pk[:, :, 0:ROWS] = jnp.where(sixth, square_sums[None], sums)

    def share_copies(src_of, dst, ss, rs):
        return [
            remote(src_of(add_mod(share, r, 16)), dst.at[share], ss.at[r - 1], rs.at[r - 1],
                   share_device(add_mod(share, r, 16)))
            for r in range(1, 16)
        ]

    pk_copies = share_copies(lambda to: pk.at[to], pk_in, pk_ss, pk_rs)
    for copy in pk_copies:
        copy.start()
    pk_in[share] = pk[share]
    for r in range(1, 16):
        arrived(pk_in.at[add_mod(share, -r, 16)], pk_rs.at[r - 1])

    def branch_value(branch):
        got = pk_in[branch]
        for i in range(1, 8):
            got = got + pk_in[2 * i + branch]
        mean = got[4:5, 0:ROWS] / D
        inv_std = lax.rsqrt(got[5:6, 0:ROWS] / D - mean * mean + EPSILON)
        return (
            inv_std * (got[0:4, 0:ROWS] - mean * got[0:4, ROWS:ROWS + 1])
            + got[0:4, ROWS + 1:ROWS + 2]
        )

    cond, uncond = branch_value(0), branch_value(1)
    guide = jnp.where(e == 0, GUIDE_HIGH, GUIDE_LOW)
    guided = uncond + guide * (cond - uncond)
    step_now = jnp.full((4, ROWS), step_ref[0], jnp.int32).astype(jnp.float32)
    delta = noise_level(1.0 - (step_now + 1.0) / STEPS) - noise_level(1.0 - step_now / STEPS)
    swap[0:4, 0:ROWS] = lat[share][0:4, :] + delta * guided
    swap_copy = remote(swap, swap_in, sw_ss, sw_rs, {"expert": 1 - e})
    swap_copy.start()
    fin[share, 0:4, 0:ROWS] = guided
    arrived(swap_in, sw_rs)
    fin[share, 4:8, 0:ROWS] = swap_in[0:4, 0:ROWS]
    fin_copies = share_copies(lambda to: fin.at[share], fin, fin_ss, fin_rs)
    for copy in fin_copies:
        copy.start()
    for r in range(1, 16):
        arrived(fin.at[add_mod(share, -r, 16)], fin_rs.at[r - 1])
    for i in range(16):
        vel_ref[4 * i:4 * i + 4, :] = fin[i, 0:4, 0:ROWS]
        rel_ref[4 * i:4 * i + 4, :] = fin[i, 4:8, 0:ROWS]

    for copy in msg_copies + pk_copies + fin_copies + [swap_copy, px_copy]:
        copy.wait_send()
    sent_all(v_copies + k_copies + q_copies)
    pl.when(jnp.logical_not(w_stays_mid))(w_mid_far.wait_send)
    pl.when(jnp.logical_not(w_stays))(w_far.wait_send)
    for copy in w_sent.values():
        copy.wait_send()
    for _, _, _, copy in ag_starts:
        copy.wait_send()
    for _, h, way, copy in ag_lasts:
        if ag_last(way, h):
            copy.wait_send()
        else:
            pl.when(holds)(copy.wait_send)

    @pl.when(attends)
    def _():
        def one(i, carry):
            relay(values, i, vr_ss, vr_rs).wait_send()
            relay(keys, i, kr_ss, kr_rs).wait_send()
            pl.when(jnp.logical_not(jnp.logical_and(i == z, holds)))(o_far(i).wait_send)
            return carry

        lax.fori_loop(0, 8, one, 0)


def local(
    query_raw,
    key_raw,
    value_rows,
    residual,
    latent,
    query_gain,
    key_gain,
    out_weight,
    attn_gate,
    head_shift,
    head_scale,
    head_weight,
    head_bias,
    valid_rows,
    step_index,
):
    vmem = pl.BlockSpec(memory_space=pltpu.VMEM)
    smem = pl.BlockSpec(memory_space=pltpu.SMEM)
    dma = pltpu.SemaphoreType.DMA
    f32, bf16 = jnp.float32, jnp.bfloat16
    hidden, velocity, relayed = pl.pallas_call(
        kernel,
        out_shape=(
            jax.ShapeDtypeStruct((ROWS, WIDTH), bf16),
            jax.ShapeDtypeStruct((64, ROWS), f32),
            jax.ShapeDtypeStruct((64, ROWS), f32),
        ),
        in_specs=[vmem] * 13 + [smem] * 2,
        out_specs=(vmem, vmem, vmem),
        scratch_shapes=[
            pltpu.VMEM((256, HD), f32),
            pltpu.VMEM((8, HD), f32),
            pltpu.VMEM((7, 8, HD), f32),
            pltpu.VMEM((ROWS, HD), f32),
            pltpu.VMEM((ROWS, HD), f32),
            pltpu.VMEM((LOCAL_HEADS, ROWS, HD), bf16),
            pltpu.VMEM((LOCAL_HEADS, ROWS, HD), bf16),
            pltpu.VMEM((TOKENS, HD), bf16),
            pltpu.VMEM((TOKENS, HD), bf16),
            pltpu.VMEM((8, ROWS, HD), bf16),
            pltpu.VMEM((1, TOKENS), f32),
            pltpu.VMEM((ROWS, TOKENS), f32),
            pltpu.VMEM((8, ROWS, HD), bf16),
            pltpu.VMEM((4, 2, ROWS, WIDTH), bf16),
            pltpu.VMEM((COLS, WIDTH), bf16),
            pltpu.VMEM((4, WIDTH, WIDTH), bf16),
            pltpu.VMEM((ROWS, WIDTH), f32),
            pltpu.VMEM((ROWS, WIDTH), bf16),
            pltpu.VMEM((ROWS, WIDTH), bf16),
            pltpu.VMEM((128, WIDTH), f32),
            pltpu.VMEM((1, HD), f32),
            pltpu.VMEM((16, 4, ROWS), f32),
            pltpu.VMEM((16, 8, 256), f32),
            pltpu.VMEM((16, 8, 256), f32),
            pltpu.VMEM((8, 256), f32),
            pltpu.VMEM((8, 256), f32),
            pltpu.VMEM((16, 8, 256), f32),
            dma((7,)), dma((7,)),
            dma((5,)), dma((8,)),
            dma((5,)), dma((8,)),
            dma((5,)), dma((8,)),
            dma((8,)), dma((8,)),
            dma((8,)), dma((8,)),
            dma((8,)), dma((2, 5)),
            dma((2, 2, 10)), dma((2, 2, 10)),
            dma, dma,
            dma, dma,
            dma((W_COPIES,)), dma((W_COPIES,)),
            dma, dma,
            dma((15,)), dma((15,)),
            dma, dma,
            dma((15,)), dma((15,)),
        ],
        compiler_params=pltpu.CompilerParams(
            collective_id=0, has_side_effects=True, vmem_limit_bytes=56 * 1024 * 1024
        ),
    )(
        query_raw[0, 0], key_raw[0, 0], value_rows[0, 0], residual[0, 0], query_gain, key_gain,
        out_weight[0].T, attn_gate, head_scale, head_shift, head_weight[0].T, head_bias,
        latent[0].T, valid_rows, step_index,
    )
    return (hidden[None, None], velocity.T[None], relayed.T[None])


def solution(mesh):
    placed = (
        P("expert", "branch", "seq", "tensor"),
        P("expert", "branch", "seq", "tensor"),
        P("expert", "branch", "seq", "tensor"),
        P("expert", "branch", "seq", "tensor"),
        P("expert", "seq", None),
        P("expert", "tensor"),
        P("expert", "tensor"),
        P("expert", "tensor", ("branch", "seq")),
        P("expert", "tensor"),
        P("expert", "tensor"),
        P("expert", "tensor"),
        P("expert", "tensor", None),
        P("expert", None),
        P("expert"),
        P("expert"),
    )
    return jax.shard_map(
        local,
        mesh=mesh,
        in_specs=placed,
        out_specs=(
            P("expert", "branch", "seq", "tensor"),
            P("expert", "seq", None),
            P("expert", "seq", None),
        ),
        check_vma=False,
    )
```

```python
import math

import jax
import jax.numpy as jnp
from jax import lax
from jax.experimental import pallas as pl
from jax.experimental.pallas import tpu as pltpu
from jax.sharding import PartitionSpec as P

D = 5120
HD = 128
GRID_H = 30
GRID_W = 52
STEPS = 40
TOKENS = 2816
EPSILON = 1e-06
THETA = 10000.0
FLOW_SHIFT = 12.0
GUIDE_HIGH = 4.0
GUIDE_LOW = 3.0
MASKED = -1e30

ROWS = 176
WIDTH = 640
COLS = 160
LOCAL_HEADS = 5
HEAD_Z = (0, 1, 3, 4, 6)
UPPER = 96
W_COPIES = 31
LIVE_FROM = 1280
MESH = pl.DeviceIdType.MESH
LOG2E = 1.4426950408889634


def add_mod(value, step, size):
    return lax.rem(value + (step % size), size)


def rope_tables(first_position):
    half_pairs = HD // 2
    third_pairs = half_pairs // 3
    first_pairs = half_pairs - 2 * third_pairs
    frame_tokens = GRID_H * GRID_W
    position = first_position + lax.broadcasted_iota(jnp.int32, (ROWS, HD), 0)
    frame = (position >= frame_tokens).astype(jnp.int32)
    for later in range(2, (TOKENS - 1) // frame_tokens + 1):
        frame = frame + (position >= later * frame_tokens).astype(jnp.int32)
    inside = (position - frame * frame_tokens).astype(jnp.float32)
    row = jnp.floor((inside + 0.5) * (1.0 / GRID_W))
    col = inside - row * GRID_W
    lane = lax.broadcasted_iota(jnp.int32, (ROWS, HD), 1)
    pair = lax.shift_right_logical(lane, 1)
    in_time = pair < first_pairs
    in_rows = pair < first_pairs + third_pairs
    offset = jnp.where(in_time, 0, jnp.where(in_rows, first_pairs, first_pairs + third_pairs))
    count = jnp.where(in_time, float(first_pairs), float(third_pairs))
    rates = jnp.exp(-math.log(THETA) * (pair - offset).astype(jnp.float32) / count)
    coords = jnp.where(in_time, frame.astype(jnp.float32), jnp.where(in_rows, row, col))
    angles = coords * rates
    odd = jnp.bitwise_and(lane, 1) == 1
    sines = jnp.sin(angles)
    return jnp.cos(angles), jnp.where(odd, sines, -sines), odd


def noise_level(frac):
    return FLOW_SHIFT * frac / (1.0 + (FLOW_SHIFT - 1.0) * frac)


def kernel(
    q_hbm, k_hbm, v_ref, res_hbm, qg_hbm, kg_hbm, w_ref, gate_hbm, scale_hbm,
    shift_hbm, hw_hbm, bias_hbm, lat_hbm, valid_ref, step_ref,
    hid_hbm, vel_hbm, rel_hbm,
    q_ref, k_ref, res_ref, qg_ref, kg_ref, gate_ref, scale_ref, shift_ref, hw_ref, bias_ref,
    lat_ref, hid_ref, vel_ref, rel_ref, in_sem, out_sem,
    sq_pad, msg, msg_in, cos, sin, qr, kr, keys, values, queries, mask, logits, outs, att, w_mid, wg, total, px, px_in,
    head_w, bias_row, lat, pk, pk_in, swap, swap_in, fin,
    msg_ss, msg_rs, v_ss, v_rs, k_ss, k_rs, q_ss, q_rs, vr_ss, vr_rs, kr_ss, kr_rs, o_ss, o_rs,
    ag_ss, ag_rs, wm_ss, wm_rs, wp_ss, wp_rs, w_ss, w_rs, px_ss, px_rs, pk_ss, pk_rs, sw_ss, sw_rs,
    fin_ss, fin_rs,
):
    e = lax.axis_index("expert")
    b = lax.axis_index("branch")
    s = lax.axis_index("seq")
    y = lax.axis_index("tensor")
    z = lax.div(s, 2)
    x_lo = lax.rem(s, 2)
    share = 2 * y + b

    def remote(src, dst, send_sem, recv_sem, device):
        return pltpu.make_async_remote_copy(
            src_ref=src, dst_ref=dst, send_sem=send_sem, recv_sem=recv_sem,
            device_id=device, device_id_type=MESH,
        )

    def arrived(ref, sem):
        pltpu.make_async_copy(ref, ref, sem).wait()

    def z_device(where):
        return {"seq": 2 * where + x_lo}

    def share_device(where):
        return {"branch": lax.rem(where, 2), "tensor": lax.div(where, 2)}

    z_up, z_down = add_mod(z, 1, 8), add_mod(z, -1, 8)
    y_up, y_down = add_mod(y, 1, 8), add_mod(y, -1, 8)
    beside = {"seq": s + 1 - 2 * x_lo}

    across = {"branch": 1 - b, "seq": 2 * z + 1 - x_lo}
    holds = lax.rem(y + b, 2) == 0
    off = lax.rem(y + b, 2)

    mid_z = 2 * lax.rem(lax.div(y, 2) + 4 - lax.div(z, 2), 4) + lax.rem(z, 2)
    to_y = 4 * b + lax.div(mid_z, 2)
    w_turns = lax.rem(y, 2) != b
    w_to = {
        "branch": lax.rem(y, 2),
        "seq": 2 * z + jnp.where(w_turns, 1 - x_lo, x_lo),
        "tensor": to_y,
    }
    turned = lax.div(y, 4) != b
    w_from = {
        "branch": lax.div(y, 4),
        "seq": 2 * z + jnp.where(turned, 1 - x_lo, x_lo),
        "tensor": 2 * lax.rem(lax.div(z, 2) + y, 4) + b,
    }
    w_stays_mid = mid_z == z
    w_stays = jnp.logical_and(lax.rem(y, 2) == b, to_y == y)

    loads = {}
    for at, (name, src, dst) in enumerate((
        ("q", q_hbm, q_ref), ("k", k_hbm, k_ref), ("scale", scale_hbm, scale_ref),
        ("shift", shift_hbm, shift_ref), ("hw", hw_hbm, hw_ref), ("bias", bias_hbm, bias_ref),
        ("lat", lat_hbm, lat_ref), ("kg", kg_hbm, kg_ref), ("qg", qg_hbm, qg_ref),
        ("gate", gate_hbm, gate_ref), ("res", res_hbm, res_ref),
    )):
        loads[name] = pltpu.make_async_copy(src, dst, in_sem.at[at])
        loads[name].start()

    barrier = pltpu.get_barrier_semaphore()

    def greet(device):
        pl.semaphore_signal(barrier, inc=1, device_id=device, device_id_type=MESH)

    for step in range(1, 8):
        greet(z_device(add_mod(z, step, 8)))
    for step in range(8):
        greet({"branch": 1 - b, "seq": 2 * add_mod(z, step, 8) + 1 - x_lo})
    for step in range(1, 16):
        greet(share_device(add_mod(share, step, 16)))
    greet(beside)
    greet({"expert": 1 - e})
    pl.when(jnp.logical_not(w_stays))(lambda: greet(w_from))

    def squares(ref):
        summed = jnp.zeros((ROWS, HD), jnp.float32)
        for h in range(LOCAL_HEADS):
            part = ref[:, h * HD:(h + 1) * HD].astype(jnp.float32)
            summed = summed + part * part
        sq_pad[0:ROWS, :] = summed
        return jnp.sum(sq_pad[...].T, axis=0, keepdims=True)

    sq_pad[ROWS:, :] = jnp.zeros((256 - ROWS, HD), jnp.float32)
    msg[...] = jnp.zeros_like(msg)
    loads["q"].wait()
    loads["k"].wait()
    for at, ref in enumerate((q_ref, k_ref)):
        row = squares(ref)
        msg[2 * at:2 * at + 1, :] = row[:, 0:HD]
        msg[2 * at + 1:2 * at + 2, :] = row[:, HD:]

    pl.semaphore_wait(barrier, 33 - w_stays.astype(jnp.int32))

    w_mid_far = remote(w_ref, w_mid, wm_ss, wm_rs, z_device(mid_z))
    w_mid_near = pltpu.make_async_copy(w_ref, w_mid, wm_rs)
    pl.when(w_stays_mid)(w_mid_near.start)
    pl.when(jnp.logical_not(w_stays_mid))(w_mid_far.start)

    msg_copies = [
        remote(msg, msg_in.at[i - 1], msg_ss.at[i - 1], msg_rs.at[i - 1],
               {"tensor": add_mod(y, i, 8)})
        for i in range(1, 8)
    ]
    for copy in msg_copies:
        copy.start()

    my_rows = pl.ds(pl.multiple_of(s * ROWS, 16), ROWS)

    def to_head(src_of, place, ss, rs):
        copies = []
        for h in range(LOCAL_HEADS):
            copies.append((
                z == HEAD_Z[h],
                pltpu.make_async_copy(src_of(h), place, rs.at[z]),
                remote(src_of(h), place, ss.at[h], rs.at[z], z_device(HEAD_Z[h])),
            ))
        return copies

    def start_all(copies):
        for here, local_copy, far in copies:
            pl.when(here)(local_copy.start)
            pl.when(jnp.logical_not(here))(far.start)

    def sent_all(copies):
        for here, _, far in copies:
            pl.when(jnp.logical_not(here))(far.wait_send)

    v_copies = to_head(lambda h: v_ref.at[:, pl.ds(h * HD, HD)], values.at[my_rows, :], v_ss, v_rs)
    k_copies = to_head(lambda h: kr.at[h], keys.at[my_rows, :], k_ss, k_rs)
    q_copies = to_head(lambda h: qr.at[h], queries.at[z], q_ss, q_rs)
    start_all(v_copies)

    cos_table, sin_table, odd = rope_tables(s * ROWS)
    cos[...] = cos_table
    sin[...] = sin_table
    limit = valid_ref[0] * GRID_W
    key_at = lax.broadcasted_iota(jnp.int32, (1, TOKENS), 1)
    mask[...] = jnp.where(key_at < limit, 0.0, MASKED)
    for name in ("scale", "shift", "hw", "bias", "lat", "kg", "qg"):
        loads[name].wait()
    bias_row[...] = jnp.zeros_like(bias_row)
    bias_row[:, 0:64] = bias_ref[...]
    bias_col = jnp.broadcast_to(bias_row[...], (HD, HD)).T[0:64, 0:1]
    weight_f = hw_ref[...].astype(jnp.float32)
    scaled = weight_f * (1.0 + scale_ref[...])
    head_u = jnp.sum(scaled, axis=1, keepdims=True)
    head_c = jnp.sum(weight_f * shift_ref[...], axis=1, keepdims=True)
    head_c = head_c + jnp.where(y == 0, bias_col, 0.0)
    lane = lax.broadcasted_iota(jnp.int32, (64, HD), 1)
    extra = jnp.where(lane == ROWS - HD, head_u, jnp.where(lane == ROWS - HD + 1, head_c, 0.0))
    head_w[...] = jnp.zeros_like(head_w)
    pk[...] = jnp.zeros_like(pk)
    swap[...] = jnp.zeros_like(swap)
    fin[...] = jnp.zeros_like(fin)
    for i in range(16):
        head_w[8 * i:8 * i + 4, :] = scaled[4 * i:4 * i + 4, :]
        head_w[8 * i + 4:8 * i + 5, :] = jnp.ones((1, WIDTH), jnp.float32)
        pk[i, 0:4, HD:] = extra[4 * i:4 * i + 4, :]
        lat[i, 0:4, :] = lat_ref[4 * i:4 * i + 4, :]

    for i in range(7):
        arrived(msg_in.at[i], msg_rs.at[i])
    sums = msg[...]
    for i in range(7):
        sums = sums + msg_in[i]
    inverse = lax.rsqrt(sums / D + EPSILON)

    def normalize_rotate(ref, gain_ref, first, out):
        column = jnp.concatenate(
            [
                jnp.broadcast_to(inverse[first:first + 1, :], (HD, HD)).T,
                jnp.broadcast_to(inverse[first + 1:first + 2, :], (HD, HD)).T[0:ROWS - HD, :],
            ],
            axis=0,
        )
        for h in range(LOCAL_HEADS):
            part = ref[:, h * HD:(h + 1) * HD].astype(jnp.float32)
            part = part * column * gain_ref[:, h * HD:(h + 1) * HD]
            swapped = jnp.where(odd, pltpu.roll(part, 1, 1), pltpu.roll(part, HD - 1, 1))
            out[h] = (part * cos[...] + swapped * sin[...]).astype(jnp.bfloat16)

    normalize_rotate(k_ref, kg_ref, 2, kr)
    start_all(k_copies)
    normalize_rotate(q_ref, qg_ref, 0, qr)
    start_all(q_copies)

    slots = {}
    base_x = jnp.where(turned, 1 - x_lo, x_lo)
    for dz in range(8):
        at_z = add_mod(z, dz, 8)
        at = lax.rem(lax.div(at_z, 2) + y, 4)
        for dx in range(2):
            at_x = 1 - base_x if dx else base_x
            slots[dz, dx] = (at, (2 * lax.rem(at_z, 2) + at_x) * COLS)

    def w_slot(dz, dx, first=0, count=COLS):
        at, row = slots[dz % 8, dx]
        return wg.at[at, pl.ds(pl.multiple_of(row + first, 16), count), :]

    def upper(dz, dx):
        return w_slot(dz, dx, 0, UPPER)

    def lower(dz, dx):
        return w_slot(dz, dx, UPPER, COLS - UPPER)

    def upper_half(dz, way):
        return w_slot(dz, 0, way * (UPPER // 2), UPPER // 2)

    w_sent, w_index = {}, {}

    def w_copy(key, block, device):
        at = w_index.setdefault(key, len(w_index))
        w_sent[key] = remote(block, block, w_ss.at[at], w_rs.at[at], device)

    def w_wait(key, block):
        arrived(block, w_rs.at[w_index[key]])

    z_to = (z_device(z_up), z_device(z_down))

    def ring_slot(j):
        k = (j + 1) // 2
        return k if j % 2 else -k

    for way in range(2):
        sign = 1 if way else -1
        for k in range(1, 5):
            held = sign * (k - 1)
            w_copy(("z", k, way), upper(held, 0) if k < 4 else upper_half(held, way), z_to[way])
            for dx in range(2):
                if k < 4 or dx == way:
                    w_copy(("lz", k, way, dx), lower(held, dx), z_to[way])
    w_copy("lx", lower(0, 0), beside)
    for j in range(8):
        w_copy(("ux", j), upper(ring_slot(j), 0), beside)

    w_near = pltpu.make_async_copy(w_mid, w_slot(0, 0), wp_rs)
    to_row = (2 * lax.rem(z, 2) + x_lo) * COLS
    w_far = remote(
        w_mid, wg.at[lax.div(y, 2), pl.ds(pl.multiple_of(to_row, 16), COLS), :], wp_ss, wp_rs,
        w_to,
    )

    def w_event(name):
        if name == "along y":
            arrived(w_mid, wm_rs)
            pl.when(w_stays)(w_near.start)
            pl.when(jnp.logical_not(w_stays))(w_far.start)
        elif name == "start":
            arrived(w_slot(0, 0), wp_rs)
            w_sent["lx"].start()
            for way in range(2):
                w_sent["z", 1, way].start()
            for way in range(2):
                w_sent["lz", 1, way, 0].start()
            w_sent["ux", 0].start()
        elif name == "lower":
            w_wait("lx", lower(0, 1))
            for way in range(2):
                w_sent["lz", 1, way, 1].start()
        elif name == "end":
            for way in range(2):
                w_wait(("z", 4, way), upper_half(4, way))
            w_sent["ux", 7].start()
        elif name == "finish":
            for dx in range(2):
                w_wait(("lz", 4, dx, dx), lower(4, dx))
            for j in range(8):
                w_wait(("ux", j), upper(ring_slot(j), 1))
        else:
            k = name
            for way in (1, 0):
                held = k if way else -k
                w_wait(("z", k, way), upper(held, 0))
                w_sent["z", k + 1, way].start()
                w_sent["ux", 2 * k - way].start()
            for dx in range(2):
                for way in (1, 0):
                    w_wait(("lz", k, way, dx), lower(k if way else -k, dx))
                    if k < 3 or dx == way:
                        w_sent["lz", k + 1, way, dx].start()

    attends = z == HEAD_Z[0]
    head = jnp.int32(0)
    for h in range(1, LOCAL_HEADS):
        attends = jnp.logical_or(attends, z == HEAD_Z[h])
        head = head + (z >= HEAD_Z[h]).astype(jnp.int32)
    head_cols = pl.ds(pl.multiple_of(head * HD, HD), HD)
    att_place = att.at[lax.div(y, 2), b, :, head_cols]

    def block_rows(buf, at_z, at_x):
        return buf.at[pl.ds(pl.multiple_of((2 * at_z + at_x) * ROWS, 16), ROWS), :]

    def relay(buf, at_z, ss, rs):
        block = block_rows(buf, at_z, x_lo)
        return remote(block, block, ss.at[at_z], rs.at[at_z], beside)

    def pass_on(buf, came, ss, rs):
        @pl.when(attends)
        def _():
            def one(i, carry):
                arrived(block_rows(buf, i, x_lo), came.at[i])
                relay(buf, i, ss, rs).start()
                return carry

            lax.fori_loop(0, 8, one, 0)

    pass_on(values, v_rs, vr_ss, vr_rs)
    w_event('along y')
    pass_on(keys, k_rs, kr_ss, kr_rs)

    @pl.when(attends)
    def _():
        def one(i, carry):
            arrived(queries.at[i], q_rs.at[i])
            arrived(block_rows(keys, i, 1 - x_lo), kr_rs.at[i])
            arrived(block_rows(values, i, 1 - x_lo), vr_rs.at[i])
            return carry

        lax.fori_loop(0, 8, one, 0)

    def o_far(at_z):
        return remote(
            outs.at[at_z], att_place, o_ss.at[at_z], o_rs.at[b, head],
            {"branch": lax.rem(y, 2), "seq": 2 * at_z + jnp.where(holds, x_lo, 1 - x_lo)},
        )

    factor = HD ** -0.5 * LOG2E

    def attend(at_z):
        query = queries[at_z]
        peak = None
        for c in range(TOKENS // 256):
            cols = slice(c * 256, (c + 1) * 256)
            part = lax.dot_general(
                query, keys[cols, :], (((1,), (1,)), ((), ())),
                preferred_element_type=jnp.float32,
            )
            if c * 256 >= LIVE_FROM:
                part = part + mask[:, cols]
            logits[:, cols] = part
            top = jnp.maximum(part[:, 0:HD], part[:, HD:])
            peak = top if peak is None else jnp.maximum(peak, top)
        peak = jnp.max(peak, axis=1, keepdims=True)
        summed = jnp.zeros((ROWS, HD), jnp.float32)
        mixed = jnp.zeros((ROWS, HD), jnp.float32)
        for c in range(TOKENS // 256):
            cols = slice(c * 256, (c + 1) * 256)
            prob = jnp.exp2((logits[:, cols] - peak) * factor)
            summed = summed + (prob[:, 0:HD] + prob[:, HD:])
            mixed = mixed + jnp.dot(
                prob.astype(jnp.bfloat16), values[cols, :], preferred_element_type=jnp.float32
            )
        denom = jnp.sum(summed, axis=1, keepdims=True)
        outs[at_z] = (mixed / denom).astype(jnp.bfloat16)

    def one_block(j, carry):
        away = lax.div(8 - j, 2)
        at_z = lax.rem(z + jnp.where(lax.rem(j, 2) == 1, away, 8 - away), 8)

        @pl.when(attends)
        def _():
            attend(at_z)
            stays = jnp.logical_and(at_z == z, holds)
            pl.when(stays)(pltpu.make_async_copy(outs.at[at_z], att_place, o_rs.at[b, head]).start)
            pl.when(jnp.logical_not(stays))(o_far(at_z).start)

        for turn, event in ((0, 'start'), (2, 'lower'), (5, 1)):
            pl.when(j == turn)(lambda: w_event(event))
        return carry

    lax.fori_loop(0, 8, one_block, 0)

    def ag_block(way, away, token_branch, h):
        at_y = lax.rem(y + (away if way else 8 - away), 8)
        return att.at[lax.div(at_y, 2), token_branch, :, pl.ds(h * HD, HD)]

    def ag_last(way, h):
        return h >= 3 if way else h < 3

    ag_starts, ag_lasts = [], []
    for which in range(2):
        for h in range(LOCAL_HEADS):
            at = LOCAL_HEADS * which + h
            tb = b if which else 1 - b
            for way in range(2):
                device = {"tensor": y_down if way else y_up}
                near = ag_block(way, off, tb, h)
                ag_starts.append((which, h, way, remote(
                    near, near, ag_ss.at[way, 0, at], ag_rs.at[way, 0, at], device)))
                far = ag_block(way, off + 2, tb, h)
                ag_lasts.append((which, h, way, remote(
                    far, far, ag_ss.at[way, 1, at], ag_rs.at[way, 1, at], device)))

    def ag_start(which):
        for part, h, way, copy in ag_starts:
            if part != which:
                continue
            at = LOCAL_HEADS * which + h
            tb = b if which else 1 - b
            if way == 0:
                place = att.at[lax.div(y, 2), tb, :, pl.ds(h * HD, HD)]
                pl.when(holds)(lambda: arrived(place, o_rs.at[tb, h]))
            near = ag_block(way, off, tb, h)
            pl.when(jnp.logical_not(holds))(lambda: arrived(near, ag_rs.at[way, 0, at]))
            copy.start()

    def ag_go_on(which):
        for part, h, way, copy in ag_lasts:
            if part != which:
                continue
            at = LOCAL_HEADS * which + h
            arrived(ag_block(way, off + 2, b if which else 1 - b, h), ag_rs.at[way, off, at])
            if ag_last(way, h):
                copy.start()
            else:
                pl.when(holds)(copy.start)

    def ag_finish(which):
        @pl.when(holds)
        def _():
            for h in range(LOCAL_HEADS):
                way = 0 if ag_last(0, h) else 1
                opposite = ag_block(way, 4, b if which else 1 - b, h)
                arrived(opposite, ag_rs.at[way, 1, LOCAL_HEADS * which + h])

    def project(tb):
        def one_group(g, carry):
            part = lax.dot_general(
                att[g, tb], wg[g], (((1,), (1,)), ((), ())), preferred_element_type=jnp.float32
            )
            total[...] += part
            return carry

        total[...] = jnp.zeros_like(total)
        lax.fori_loop(0, 4, one_group, 0)
        return total[...]

    ag_start(0)
    w_event(2)
    ag_start(1)
    w_event(3)
    ag_go_on(0)
    w_event('end')
    ag_go_on(1)
    ag_finish(0)
    w_event('finish')
    px[...] = project(1 - b).astype(jnp.bfloat16)
    px_copy = remote(px, px_in, px_ss, px_rs, across)
    px_copy.start()
    ag_finish(1)
    projected = project(b)
    arrived(px_in, px_rs)
    projected = projected + px_in[...].astype(jnp.float32)
    loads["gate"].wait()
    loads["res"].wait()
    hidden = (res_ref[...].astype(jnp.float32) + gate_ref[...] * projected).astype(jnp.bfloat16)
    hid_ref[...] = hidden
    hid_out = pltpu.make_async_copy(hid_ref, hid_hbm, out_sem.at[0])
    hid_out.start()
    hidden_f = hidden.astype(jnp.float32)

    over_features = (((1,), (1,)), ((), ()))
    sums = lax.dot_general(
        head_w[...], hidden_f, over_features, precision=lax.Precision.HIGHEST,
        preferred_element_type=jnp.float32,
    ).reshape(16, 8, ROWS)
    square_sums = lax.dot_general(
        jnp.ones((8, WIDTH), jnp.float32), hidden_f * hidden_f, over_features,
        precision=lax.Precision.HIGHEST, preferred_element_type=jnp.float32,
    )
    sixth = lax.broadcasted_iota(jnp.int32, (16, 8, ROWS), 1) == 5
    pk[:, :, 0:ROWS] = jnp.where(sixth, square_sums[None], sums)

    def share_copies(src_of, dst, ss, rs):
        return [
            remote(src_of(add_mod(share, r, 16)), dst.at[share], ss.at[r - 1], rs.at[r - 1],
                   share_device(add_mod(share, r, 16)))
            for r in range(1, 16)
        ]

    pk_copies = share_copies(lambda to: pk.at[to], pk_in, pk_ss, pk_rs)
    for copy in pk_copies:
        copy.start()
    pk_in[share] = pk[share]
    for r in range(1, 16):
        arrived(pk_in.at[add_mod(share, -r, 16)], pk_rs.at[r - 1])

    def branch_value(branch):
        got = pk_in[branch]
        for i in range(1, 8):
            got = got + pk_in[2 * i + branch]
        mean = got[4:5, 0:ROWS] / D
        inv_std = lax.rsqrt(got[5:6, 0:ROWS] / D - mean * mean + EPSILON)
        return (
            inv_std * (got[0:4, 0:ROWS] - mean * got[0:4, ROWS:ROWS + 1])
            + got[0:4, ROWS + 1:ROWS + 2]
        )

    cond, uncond = branch_value(0), branch_value(1)
    guide = jnp.where(e == 0, GUIDE_HIGH, GUIDE_LOW)
    guided = uncond + guide * (cond - uncond)
    step_now = jnp.full((4, ROWS), step_ref[0], jnp.int32).astype(jnp.float32)
    delta = noise_level(1.0 - (step_now + 1.0) / STEPS) - noise_level(1.0 - step_now / STEPS)
    swap[0:4, 0:ROWS] = lat[share][0:4, :] + delta * guided
    swap_copy = remote(swap, swap_in, sw_ss, sw_rs, {"expert": 1 - e})
    swap_copy.start()
    fin[share, 0:4, 0:ROWS] = guided
    arrived(swap_in, sw_rs)
    fin[share, 4:8, 0:ROWS] = swap_in[0:4, 0:ROWS]
    fin_copies = share_copies(lambda to: fin.at[share], fin, fin_ss, fin_rs)
    for copy in fin_copies:
        copy.start()
    for r in range(1, 16):
        arrived(fin.at[add_mod(share, -r, 16)], fin_rs.at[r - 1])
    for i in range(16):
        vel_ref[4 * i:4 * i + 4, :] = fin[i, 0:4, 0:ROWS]
        rel_ref[4 * i:4 * i + 4, :] = fin[i, 4:8, 0:ROWS]

    vel_out = pltpu.make_async_copy(vel_ref, vel_hbm, out_sem.at[1])
    rel_out = pltpu.make_async_copy(rel_ref, rel_hbm, out_sem.at[2])
    vel_out.start()
    rel_out.start()

    hid_out.wait()
    for copy in msg_copies + pk_copies + fin_copies + [swap_copy, px_copy]:
        copy.wait_send()
    sent_all(v_copies + k_copies + q_copies)
    pl.when(jnp.logical_not(w_stays_mid))(w_mid_far.wait_send)
    pl.when(jnp.logical_not(w_stays))(w_far.wait_send)
    for copy in w_sent.values():
        copy.wait_send()
    for _, _, _, copy in ag_starts:
        copy.wait_send()
    for _, h, way, copy in ag_lasts:
        if ag_last(way, h):
            copy.wait_send()
        else:
            pl.when(holds)(copy.wait_send)

    @pl.when(attends)
    def _():
        def one(i, carry):
            relay(values, i, vr_ss, vr_rs).wait_send()
            relay(keys, i, kr_ss, kr_rs).wait_send()
            pl.when(jnp.logical_not(jnp.logical_and(i == z, holds)))(o_far(i).wait_send)
            return carry

        lax.fori_loop(0, 8, one, 0)
    vel_out.wait()
    rel_out.wait()


def local(
    query_raw,
    key_raw,
    value_rows,
    residual,
    latent,
    query_gain,
    key_gain,
    out_weight,
    attn_gate,
    head_shift,
    head_scale,
    head_weight,
    head_bias,
    valid_rows,
    step_index,
):
    hbm = pl.BlockSpec(memory_space=pl.ANY)
    smem = pl.BlockSpec(memory_space=pltpu.SMEM)
    dma = pltpu.SemaphoreType.DMA
    f32, bf16 = jnp.float32, jnp.bfloat16
    hidden, velocity, relayed = pl.pallas_call(
        kernel,
        out_shape=(
            jax.ShapeDtypeStruct((ROWS, WIDTH), bf16),
            jax.ShapeDtypeStruct((64, ROWS), f32),
            jax.ShapeDtypeStruct((64, ROWS), f32),
        ),
        in_specs=[hbm] * 13 + [smem] * 2,
        out_specs=(hbm, hbm, hbm),
        scratch_shapes=[
            pltpu.VMEM((ROWS, WIDTH), bf16),
            pltpu.VMEM((ROWS, WIDTH), bf16),
            pltpu.VMEM((ROWS, WIDTH), bf16),
            pltpu.VMEM((1, WIDTH), f32),
            pltpu.VMEM((1, WIDTH), f32),
            pltpu.VMEM((1, WIDTH), f32),
            pltpu.VMEM((1, WIDTH), f32),
            pltpu.VMEM((1, WIDTH), f32),
            pltpu.VMEM((64, WIDTH), bf16),
            pltpu.VMEM((1, 64), f32),
            pltpu.VMEM((64, ROWS), f32),
            pltpu.VMEM((ROWS, WIDTH), bf16),
            pltpu.VMEM((64, ROWS), f32),
            pltpu.VMEM((64, ROWS), f32),
            dma((11,)), dma((3,)),
            pltpu.VMEM((256, HD), f32),
            pltpu.VMEM((8, HD), f32),
            pltpu.VMEM((7, 8, HD), f32),
            pltpu.VMEM((ROWS, HD), f32),
            pltpu.VMEM((ROWS, HD), f32),
            pltpu.VMEM((LOCAL_HEADS, ROWS, HD), bf16),
            pltpu.VMEM((LOCAL_HEADS, ROWS, HD), bf16),
            pltpu.VMEM((TOKENS, HD), bf16),
            pltpu.VMEM((TOKENS, HD), bf16),
            pltpu.VMEM((8, ROWS, HD), bf16),
            pltpu.VMEM((1, TOKENS), f32),
            pltpu.VMEM((ROWS, TOKENS), f32),
            pltpu.VMEM((8, ROWS, HD), bf16),
            pltpu.VMEM((4, 2, ROWS, WIDTH), bf16),
            pltpu.VMEM((COLS, WIDTH), bf16),
            pltpu.VMEM((4, WIDTH, WIDTH), bf16),
            pltpu.VMEM((ROWS, WIDTH), f32),
            pltpu.VMEM((ROWS, WIDTH), bf16),
            pltpu.VMEM((ROWS, WIDTH), bf16),
            pltpu.VMEM((128, WIDTH), f32),
            pltpu.VMEM((1, HD), f32),
            pltpu.VMEM((16, 4, ROWS), f32),
            pltpu.VMEM((16, 8, 256), f32),
            pltpu.VMEM((16, 8, 256), f32),
            pltpu.VMEM((8, 256), f32),
            pltpu.VMEM((8, 256), f32),
            pltpu.VMEM((16, 8, 256), f32),
            dma((7,)), dma((7,)),
            dma((5,)), dma((8,)),
            dma((5,)), dma((8,)),
            dma((5,)), dma((8,)),
            dma((8,)), dma((8,)),
            dma((8,)), dma((8,)),
            dma((8,)), dma((2, 5)),
            dma((2, 2, 10)), dma((2, 2, 10)),
            dma, dma,
            dma, dma,
            dma((W_COPIES,)), dma((W_COPIES,)),
            dma, dma,
            dma((15,)), dma((15,)),
            dma, dma,
            dma((15,)), dma((15,)),
        ],
        compiler_params=pltpu.CompilerParams(
            collective_id=0, has_side_effects=True, vmem_limit_bytes=56 * 1024 * 1024
        ),
    )(
        query_raw[0, 0], key_raw[0, 0], value_rows[0, 0], residual[0, 0], query_gain, key_gain,
        out_weight[0].T, attn_gate, head_scale, head_shift, head_weight[0].T, head_bias,
        latent[0].T, valid_rows, step_index,
    )
    return (hidden[None, None], velocity.T[None], relayed.T[None])


def solution(mesh):
    placed = (
        P("expert", "branch", "seq", "tensor"),
        P("expert", "branch", "seq", "tensor"),
        P("expert", "branch", "seq", "tensor"),
        P("expert", "branch", "seq", "tensor"),
        P("expert", "seq", None),
        P("expert", "tensor"),
        P("expert", "tensor"),
        P("expert", "tensor", ("branch", "seq")),
        P("expert", "tensor"),
        P("expert", "tensor"),
        P("expert", "tensor"),
        P("expert", "tensor", None),
        P("expert", None),
        P("expert"),
        P("expert"),
    )
    return jax.shard_map(
        local,
        mesh=mesh,
        in_specs=placed,
        out_specs=(
            P("expert", "branch", "seq", "tensor"),
            P("expert", "seq", None),
            P("expert", "seq", None),
        ),
        check_vma=False,
    )
```

```python
import math

import jax
import jax.numpy as jnp
from jax import lax
from jax.experimental import pallas as pl
from jax.experimental.pallas import tpu as pltpu
from jax.sharding import PartitionSpec as P

D = 5120
HD = 128
GRID_H = 30
GRID_W = 52
STEPS = 40
TOKENS = 2816
EPSILON = 1e-06
THETA = 10000.0
FLOW_SHIFT = 12.0
GUIDE_HIGH = 4.0
GUIDE_LOW = 3.0
MASKED = -1e30

ROWS = 176
WIDTH = 640
COLS = 160
LOCAL_HEADS = 5
HEAD_Z = (0, 1, 3, 4, 6)
UPPER = 96
W_COPIES = 31
PX_PARTS = ((0, 384), (384, 256))
LIVE_FROM = 1280
MESH = pl.DeviceIdType.MESH
LOG2E = 1.4426950408889634


def add_mod(value, step, size):
    return lax.rem(value + (step % size), size)


def rope_tables(first_position):
    half_pairs = HD // 2
    third_pairs = half_pairs // 3
    first_pairs = half_pairs - 2 * third_pairs
    frame_tokens = GRID_H * GRID_W
    position = first_position + lax.broadcasted_iota(jnp.int32, (ROWS, HD), 0)
    frame = (position >= frame_tokens).astype(jnp.int32)
    for later in range(2, (TOKENS - 1) // frame_tokens + 1):
        frame = frame + (position >= later * frame_tokens).astype(jnp.int32)
    inside = (position - frame * frame_tokens).astype(jnp.float32)
    row = jnp.floor((inside + 0.5) * (1.0 / GRID_W))
    col = inside - row * GRID_W
    lane = lax.broadcasted_iota(jnp.int32, (ROWS, HD), 1)
    pair = lax.shift_right_logical(lane, 1)
    in_time = pair < first_pairs
    in_rows = pair < first_pairs + third_pairs
    offset = jnp.where(in_time, 0, jnp.where(in_rows, first_pairs, first_pairs + third_pairs))
    count = jnp.where(in_time, float(first_pairs), float(third_pairs))
    rates = jnp.exp(-math.log(THETA) * (pair - offset).astype(jnp.float32) / count)
    coords = jnp.where(in_time, frame.astype(jnp.float32), jnp.where(in_rows, row, col))
    angles = coords * rates
    odd = jnp.bitwise_and(lane, 1) == 1
    sines = jnp.sin(angles)
    return jnp.cos(angles), jnp.where(odd, sines, -sines), odd


def noise_level(frac):
    return FLOW_SHIFT * frac / (1.0 + (FLOW_SHIFT - 1.0) * frac)


def kernel(
    q_hbm, k_hbm, v_ref, res_hbm, qg_hbm, kg_hbm, w_ref, gate_hbm, scale_hbm,
    shift_hbm, hw_hbm, bias_hbm, lat_hbm, valid_ref, step_ref,
    hid_hbm, vel_hbm, rel_hbm,
    q_ref, k_ref, res_ref, qg_ref, kg_ref, gate_ref, scale_ref, shift_ref, hw_ref, bias_ref,
    lat_ref, hid_ref, vel_ref, rel_ref, in_sem, out_sem,
    sq_pad, msg, msg_in, cos, sin, qr, kr, keys, values, queries, mask, logits, outs, att, w_mid, wg, total, px, px_in,
    head_w, bias_row, lat, pk, pk_in, swap, swap_in, fin,
    msg_ss, msg_rs, v_ss, v_rs, k_ss, k_rs, q_ss, q_rs, vr_ss, vr_rs, kr_ss, kr_rs, o_ss, o_rs,
    ag_ss, ag_rs, wm_ss, wm_rs, wp_ss, wp_rs, w_ss, w_rs, px_ss, px_rs, pk_ss, pk_rs, sw_ss, sw_rs,
    fin_ss, fin_rs,
):
    e = lax.axis_index("expert")
    b = lax.axis_index("branch")
    s = lax.axis_index("seq")
    y = lax.axis_index("tensor")
    z = lax.div(s, 2)
    x_lo = lax.rem(s, 2)
    share = 2 * y + b

    def remote(src, dst, send_sem, recv_sem, device):
        return pltpu.make_async_remote_copy(
            src_ref=src, dst_ref=dst, send_sem=send_sem, recv_sem=recv_sem,
            device_id=device, device_id_type=MESH,
        )

    def arrived(ref, sem):
        pltpu.make_async_copy(ref, ref, sem).wait()

    def z_device(where):
        return {"seq": 2 * where + x_lo}

    def share_device(where):
        return {"branch": lax.rem(where, 2), "tensor": lax.div(where, 2)}

    z_up, z_down = add_mod(z, 1, 8), add_mod(z, -1, 8)
    y_up, y_down = add_mod(y, 1, 8), add_mod(y, -1, 8)
    beside = {"seq": s + 1 - 2 * x_lo}

    across = {"branch": 1 - b, "seq": 2 * z + 1 - x_lo}
    holds = lax.rem(y + b, 2) == 0
    off = lax.rem(y + b, 2)

    pair = lax.div(z, 2)
    mid_pair = lax.rem(lax.div(y, 2) + 4 - pair, 4)
    mid_odd = jnp.where(lax.rem(mid_pair + 4 - pair, 4) == 2, 1 - lax.rem(z, 2), lax.rem(z, 2))
    mid_z = 2 * mid_pair + mid_odd
    to_y = 4 * b + lax.div(mid_z, 2)
    w_turns = lax.rem(y, 2) != b
    w_to = {
        "branch": lax.rem(y, 2),
        "seq": 2 * z + jnp.where(w_turns, 1 - x_lo, x_lo),
        "tensor": to_y,
    }
    turned = lax.div(y, 4) != b
    w_from = {
        "branch": lax.div(y, 4),
        "seq": 2 * z + jnp.where(turned, 1 - x_lo, x_lo),
        "tensor": 2 * lax.rem(lax.div(z, 2) + y, 4) + b,
    }
    w_stays_mid = mid_z == z
    w_stays = jnp.logical_and(lax.rem(y, 2) == b, to_y == y)

    loads = {}
    for at, (name, src, dst) in enumerate((
        ("q", q_hbm, q_ref), ("k", k_hbm, k_ref), ("scale", scale_hbm, scale_ref),
        ("shift", shift_hbm, shift_ref), ("hw", hw_hbm, hw_ref), ("bias", bias_hbm, bias_ref),
        ("lat", lat_hbm, lat_ref), ("kg", kg_hbm, kg_ref), ("qg", qg_hbm, qg_ref),
        ("gate", gate_hbm, gate_ref), ("res", res_hbm, res_ref),
    )):
        loads[name] = pltpu.make_async_copy(src, dst, in_sem.at[at])
        loads[name].start()

    barrier = pltpu.get_barrier_semaphore()

    def greet(device):
        pl.semaphore_signal(barrier, inc=1, device_id=device, device_id_type=MESH)

    for step in range(1, 8):
        greet(z_device(add_mod(z, step, 8)))
    for step in range(8):
        greet({"branch": 1 - b, "seq": 2 * add_mod(z, step, 8) + 1 - x_lo})
    for step in range(1, 16):
        greet(share_device(add_mod(share, step, 16)))
    greet(beside)
    greet({"expert": 1 - e})
    pl.when(jnp.logical_not(w_stays))(lambda: greet(w_from))

    def squares(ref):
        summed = jnp.zeros((ROWS, HD), jnp.float32)
        for h in range(LOCAL_HEADS):
            part = ref[:, h * HD:(h + 1) * HD].astype(jnp.float32)
            summed = summed + part * part
        sq_pad[0:ROWS, :] = summed
        return jnp.sum(sq_pad[...].T, axis=0, keepdims=True)

    sq_pad[ROWS:, :] = jnp.zeros((256 - ROWS, HD), jnp.float32)
    msg[...] = jnp.zeros_like(msg)
    loads["q"].wait()
    loads["k"].wait()
    for at, ref in enumerate((q_ref, k_ref)):
        row = squares(ref)
        msg[2 * at:2 * at + 1, :] = row[:, 0:HD]
        msg[2 * at + 1:2 * at + 2, :] = row[:, HD:]

    pl.semaphore_wait(barrier, 33 - w_stays.astype(jnp.int32))

    w_mid_far = remote(w_ref, w_mid, wm_ss, wm_rs, z_device(mid_z))
    w_mid_near = pltpu.make_async_copy(w_ref, w_mid, wm_rs)
    pl.when(w_stays_mid)(w_mid_near.start)
    pl.when(jnp.logical_not(w_stays_mid))(w_mid_far.start)

    msg_copies = [
        remote(msg, msg_in.at[i - 1], msg_ss.at[i - 1], msg_rs.at[i - 1],
               {"tensor": add_mod(y, i, 8)})
        for i in range(1, 8)
    ]
    for copy in msg_copies:
        copy.start()

    my_rows = pl.ds(pl.multiple_of(s * ROWS, 16), ROWS)

    def to_head(src_of, place, ss, rs):
        copies = []
        for h in range(LOCAL_HEADS):
            copies.append((
                z == HEAD_Z[h],
                pltpu.make_async_copy(src_of(h), place, rs.at[z]),
                remote(src_of(h), place, ss.at[h], rs.at[z], z_device(HEAD_Z[h])),
            ))
        return copies

    def start_all(copies):
        for here, local_copy, far in copies:
            pl.when(here)(local_copy.start)
            pl.when(jnp.logical_not(here))(far.start)

    def sent_all(copies):
        for here, _, far in copies:
            pl.when(jnp.logical_not(here))(far.wait_send)

    v_copies = to_head(lambda h: v_ref.at[:, pl.ds(h * HD, HD)], values.at[my_rows, :], v_ss, v_rs)
    k_copies = to_head(lambda h: kr.at[h], keys.at[my_rows, :], k_ss, k_rs)
    q_copies = to_head(lambda h: qr.at[h], queries.at[z], q_ss, q_rs)
    start_all(v_copies)

    cos_table, sin_table, odd = rope_tables(s * ROWS)
    cos[...] = cos_table
    sin[...] = sin_table
    limit = valid_ref[0] * GRID_W
    key_at = lax.broadcasted_iota(jnp.int32, (1, TOKENS), 1)
    mask[...] = jnp.where(key_at < limit, 0.0, MASKED)
    for name in ("scale", "shift", "hw", "bias", "lat", "kg", "qg"):
        loads[name].wait()
    bias_row[...] = jnp.zeros_like(bias_row)
    bias_row[:, 0:64] = bias_ref[...]
    bias_col = jnp.broadcast_to(bias_row[...], (HD, HD)).T[0:64, 0:1]
    weight_f = hw_ref[...].astype(jnp.float32)
    scaled = weight_f * (1.0 + scale_ref[...])
    head_u = jnp.sum(scaled, axis=1, keepdims=True)
    head_c = jnp.sum(weight_f * shift_ref[...], axis=1, keepdims=True)
    head_c = head_c + jnp.where(y == 0, bias_col, 0.0)
    lane = lax.broadcasted_iota(jnp.int32, (64, HD), 1)
    extra = jnp.where(lane == ROWS - HD, head_u, jnp.where(lane == ROWS - HD + 1, head_c, 0.0))
    head_w[...] = jnp.zeros_like(head_w)
    pk[...] = jnp.zeros_like(pk)
    swap[...] = jnp.zeros_like(swap)
    fin[...] = jnp.zeros_like(fin)
    for i in range(16):
        head_w[8 * i:8 * i + 4, :] = scaled[4 * i:4 * i + 4, :]
        head_w[8 * i + 4:8 * i + 5, :] = jnp.ones((1, WIDTH), jnp.float32)
        pk[i, 0:4, HD:] = extra[4 * i:4 * i + 4, :]
        lat[i, 0:4, :] = lat_ref[4 * i:4 * i + 4, :]

    for i in range(7):
        arrived(msg_in.at[i], msg_rs.at[i])
    sums = msg[...]
    for i in range(7):
        sums = sums + msg_in[i]
    inverse = lax.rsqrt(sums / D + EPSILON)

    def normalize_rotate(ref, gain_ref, first, out):
        column = jnp.concatenate(
            [
                jnp.broadcast_to(inverse[first:first + 1, :], (HD, HD)).T,
                jnp.broadcast_to(inverse[first + 1:first + 2, :], (HD, HD)).T[0:ROWS - HD, :],
            ],
            axis=0,
        )
        for h in range(LOCAL_HEADS):
            part = ref[:, h * HD:(h + 1) * HD].astype(jnp.float32)
            part = part * column * gain_ref[:, h * HD:(h + 1) * HD]
            swapped = jnp.where(odd, pltpu.roll(part, 1, 1), pltpu.roll(part, HD - 1, 1))
            out[h] = (part * cos[...] + swapped * sin[...]).astype(jnp.bfloat16)

    normalize_rotate(k_ref, kg_ref, 2, kr)
    start_all(k_copies)
    normalize_rotate(q_ref, qg_ref, 0, qr)
    start_all(q_copies)

    slots = {}
    base_x = jnp.where(turned, 1 - x_lo, x_lo)
    for dz in range(8):
        at_z = add_mod(z, dz, 8)
        at_pair = lax.div(at_z, 2)
        at = lax.rem(at_pair + y, 4)
        at_odd = lax.rem(at_z, 2)
        at_odd = jnp.where(lax.rem(at_pair + 4 - lax.rem(y, 4), 4) == 2, 1 - at_odd, at_odd)
        for dx in range(2):
            at_x = 1 - base_x if dx else base_x
            slots[dz, dx] = (at, (2 * at_odd + at_x) * COLS)

    def w_slot(dz, dx, first=0, count=COLS):
        at, row = slots[dz % 8, dx]
        return wg.at[at, pl.ds(pl.multiple_of(row + first, 16), count), :]

    def upper(dz, dx):
        return w_slot(dz, dx, 0, UPPER)

    def lower(dz, dx):
        return w_slot(dz, dx, UPPER, COLS - UPPER)

    def upper_half(dz, way):
        return w_slot(dz, 0, way * (UPPER // 2), UPPER // 2)

    w_sent, w_index = {}, {}

    def w_copy(key, block, device):
        at = w_index.setdefault(key, len(w_index))
        w_sent[key] = remote(block, block, w_ss.at[at], w_rs.at[at], device)

    def w_wait(key, block):
        arrived(block, w_rs.at[w_index[key]])

    z_to = (z_device(z_up), z_device(z_down))

    def ring_slot(j):
        k = (j + 1) // 2
        return k if j % 2 else -k

    for way in range(2):
        sign = 1 if way else -1
        for k in range(1, 5):
            held = sign * (k - 1)
            w_copy(("z", k, way), upper(held, 0) if k < 4 else upper_half(held, way), z_to[way])
            for dx in range(2):
                if k < 4 or dx == way:
                    w_copy(("lz", k, way, dx), lower(held, dx), z_to[way])
    w_copy("lx", lower(0, 0), beside)
    for j in range(8):
        w_copy(("ux", j), upper(ring_slot(j), 0), beside)

    w_near = pltpu.make_async_copy(w_mid, w_slot(0, 0), wp_rs)
    to_row = (2 * lax.rem(mid_z, 2) + x_lo) * COLS
    w_far = remote(
        w_mid, wg.at[lax.div(y, 2), pl.ds(pl.multiple_of(to_row, 16), COLS), :], wp_ss, wp_rs,
        w_to,
    )

    def w_event(name):
        if name == "along y":
            arrived(w_mid, wm_rs)
            pl.when(w_stays)(w_near.start)
            pl.when(jnp.logical_not(w_stays))(w_far.start)
        elif name == "start":
            arrived(w_slot(0, 0), wp_rs)
            w_sent["lx"].start()
            for way in range(2):
                w_sent["z", 1, way].start()
            for way in range(2):
                w_sent["lz", 1, way, 0].start()
            w_sent["ux", 0].start()
        elif name == "lower":
            w_wait("lx", lower(0, 1))
            for way in range(2):
                w_sent["lz", 1, way, 1].start()
        elif name == "end":
            for way in range(2):
                w_wait(("z", 4, way), upper_half(4, way))
            w_sent["ux", 7].start()
        elif name == "finish":
            for dx in range(2):
                w_wait(("lz", 4, dx, dx), lower(4, dx))
            for j in range(8):
                w_wait(("ux", j), upper(ring_slot(j), 1))
        else:
            k = name
            for way in (1, 0):
                held = k if way else -k
                w_wait(("z", k, way), upper(held, 0))
                w_sent["z", k + 1, way].start()
                w_sent["ux", 2 * k - way].start()
            for dx in range(2):
                for way in (1, 0):
                    w_wait(("lz", k, way, dx), lower(k if way else -k, dx))
                    if k < 3 or dx == way:
                        w_sent["lz", k + 1, way, dx].start()

    attends = z == HEAD_Z[0]
    head = jnp.int32(0)
    for h in range(1, LOCAL_HEADS):
        attends = jnp.logical_or(attends, z == HEAD_Z[h])
        head = head + (z >= HEAD_Z[h]).astype(jnp.int32)
    head_cols = pl.ds(pl.multiple_of(head * HD, HD), HD)
    att_place = att.at[lax.div(y, 2), b, :, head_cols]

    def block_rows(buf, at_z, at_x):
        return buf.at[pl.ds(pl.multiple_of((2 * at_z + at_x) * ROWS, 16), ROWS), :]

    def relay(buf, at_z, ss, rs):
        block = block_rows(buf, at_z, x_lo)
        return remote(block, block, ss.at[at_z], rs.at[at_z], beside)

    def pass_on(buf, came, ss, rs):
        @pl.when(attends)
        def _():
            def one(i, carry):
                arrived(block_rows(buf, i, x_lo), came.at[i])
                relay(buf, i, ss, rs).start()
                return carry

            lax.fori_loop(0, 8, one, 0)

    pass_on(values, v_rs, vr_ss, vr_rs)
    w_event('along y')
    pass_on(keys, k_rs, kr_ss, kr_rs)

    @pl.when(attends)
    def _():
        def one(i, carry):
            arrived(queries.at[i], q_rs.at[i])
            arrived(block_rows(keys, i, 1 - x_lo), kr_rs.at[i])
            arrived(block_rows(values, i, 1 - x_lo), vr_rs.at[i])
            return carry

        lax.fori_loop(0, 8, one, 0)

    def o_far(at_z):
        return remote(
            outs.at[at_z], att_place, o_ss.at[at_z], o_rs.at[b, head],
            {"branch": lax.rem(y, 2), "seq": 2 * at_z + jnp.where(holds, x_lo, 1 - x_lo)},
        )

    factor = HD ** -0.5 * LOG2E

    def attend(at_z):
        query = queries[at_z]
        peak = None
        for c in range(TOKENS // 256):
            cols = slice(c * 256, (c + 1) * 256)
            part = lax.dot_general(
                query, keys[cols, :], (((1,), (1,)), ((), ())),
                preferred_element_type=jnp.float32,
            )
            if c * 256 >= LIVE_FROM:
                part = part + mask[:, cols]
            logits[:, cols] = part
            top = jnp.maximum(part[:, 0:HD], part[:, HD:])
            peak = top if peak is None else jnp.maximum(peak, top)
        peak = jnp.max(peak, axis=1, keepdims=True)
        summed = jnp.zeros((ROWS, HD), jnp.float32)
        mixed = jnp.zeros((ROWS, HD), jnp.float32)
        for c in range(TOKENS // 256):
            cols = slice(c * 256, (c + 1) * 256)
            prob = jnp.exp2((logits[:, cols] - peak) * factor)
            summed = summed + (prob[:, 0:HD] + prob[:, HD:])
            mixed = mixed + jnp.dot(
                prob.astype(jnp.bfloat16), values[cols, :], preferred_element_type=jnp.float32
            )
        denom = jnp.sum(summed, axis=1, keepdims=True)
        outs[at_z] = (mixed / denom).astype(jnp.bfloat16)

    def one_block(j, carry):
        away = lax.div(8 - j, 2)
        at_z = lax.rem(z + jnp.where(lax.rem(j, 2) == 1, away, 8 - away), 8)

        @pl.when(attends)
        def _():
            attend(at_z)
            stays = jnp.logical_and(at_z == z, holds)
            pl.when(stays)(pltpu.make_async_copy(outs.at[at_z], att_place, o_rs.at[b, head]).start)
            pl.when(jnp.logical_not(stays))(o_far(at_z).start)

        for turn, event in ((0, 'start'), (2, 'lower'), (6, 1)):
            pl.when(j == turn)(lambda: w_event(event))
        return carry

    lax.fori_loop(0, 8, one_block, 0)

    def ag_block(way, away, token_branch, h):
        at_y = lax.rem(y + (away if way else 8 - away), 8)
        return att.at[lax.div(at_y, 2), token_branch, :, pl.ds(h * HD, HD)]

    def ag_last(way, h):
        return h >= 3 if way else h < 3

    ag_starts, ag_lasts = [], []
    for which in range(2):
        for h in range(LOCAL_HEADS):
            at = LOCAL_HEADS * which + h
            tb = b if which else 1 - b
            for way in range(2):
                device = {"tensor": y_down if way else y_up}
                near = ag_block(way, off, tb, h)
                ag_starts.append((which, h, way, remote(
                    near, near, ag_ss.at[way, 0, at], ag_rs.at[way, 0, at], device)))
                far = ag_block(way, off + 2, tb, h)
                ag_lasts.append((which, h, way, remote(
                    far, far, ag_ss.at[way, 1, at], ag_rs.at[way, 1, at], device)))

    def ag_start(which):
        for part, h, way, copy in ag_starts:
            if part != which:
                continue
            at = LOCAL_HEADS * which + h
            tb = b if which else 1 - b
            if way == 0:
                place = att.at[lax.div(y, 2), tb, :, pl.ds(h * HD, HD)]
                pl.when(holds)(lambda: arrived(place, o_rs.at[tb, h]))
            near = ag_block(way, off, tb, h)
            pl.when(jnp.logical_not(holds))(lambda: arrived(near, ag_rs.at[way, 0, at]))
            copy.start()

    def ag_go_on(which):
        for part, h, way, copy in ag_lasts:
            if part != which:
                continue
            at = LOCAL_HEADS * which + h
            arrived(ag_block(way, off + 2, b if which else 1 - b, h), ag_rs.at[way, off, at])
            if ag_last(way, h):
                copy.start()
            else:
                pl.when(holds)(copy.start)

    def ag_finish(which):
        @pl.when(holds)
        def _():
            for h in range(LOCAL_HEADS):
                way = 0 if ag_last(0, h) else 1
                opposite = ag_block(way, 4, b if which else 1 - b, h)
                arrived(opposite, ag_rs.at[way, 1, LOCAL_HEADS * which + h])

    def project(tb, first, count):
        parts = [
            lax.dot_general(
                att[g, tb], wg[g, first:first + count, :], (((1,), (1,)), ((), ())),
                preferred_element_type=jnp.float32,
            )
            for g in range(4)
        ]
        return (parts[0] + parts[1]) + (parts[2] + parts[3])

    ag_start(0)
    w_event(2)
    ag_start(1)
    w_event(3)
    ag_go_on(0)
    w_event('end')
    ag_go_on(1)
    ag_finish(0)
    w_event('finish')
    px_copies = []
    for at, (first, count) in enumerate(PX_PARTS):
        cols = pl.ds(first, count)
        px[:, first:first + count] = project(1 - b, first, count).astype(jnp.bfloat16)
        copy = remote(px.at[:, cols], px_in.at[:, cols], px_ss.at[at], px_rs.at[at], across)
        copy.start()
        px_copies.append(copy)
    ag_finish(1)
    for first, count in PX_PARTS:
        total[:, first:first + count] = project(b, first, count)
    for at, (first, count) in enumerate(PX_PARTS):
        arrived(px_in.at[:, pl.ds(first, count)], px_rs.at[at])
    projected = total[...] + px_in[...].astype(jnp.float32)
    loads["gate"].wait()
    loads["res"].wait()
    hidden = (res_ref[...].astype(jnp.float32) + gate_ref[...] * projected).astype(jnp.bfloat16)
    hid_ref[...] = hidden
    hid_out = pltpu.make_async_copy(hid_ref, hid_hbm, out_sem.at[0])
    hid_out.start()
    hidden_f = hidden.astype(jnp.float32)

    over_features = (((1,), (1,)), ((), ()))
    sums = lax.dot_general(
        head_w[...], hidden_f, over_features, precision=lax.Precision.HIGHEST,
        preferred_element_type=jnp.float32,
    ).reshape(16, 8, ROWS)
    square_sums = lax.dot_general(
        jnp.ones((8, WIDTH), jnp.float32), hidden_f * hidden_f, over_features,
        precision=lax.Precision.HIGHEST, preferred_element_type=jnp.float32,
    )
    sixth = lax.broadcasted_iota(jnp.int32, (16, 8, ROWS), 1) == 5
    pk[:, :, 0:ROWS] = jnp.where(sixth, square_sums[None], sums)

    def share_copies(src_of, dst, ss, rs):
        return [
            remote(src_of(add_mod(share, r, 16)), dst.at[share], ss.at[r - 1], rs.at[r - 1],
                   share_device(add_mod(share, r, 16)))
            for r in range(1, 16)
        ]

    pk_copies = share_copies(lambda to: pk.at[to], pk_in, pk_ss, pk_rs)
    for copy in pk_copies:
        copy.start()
    pk_in[share] = pk[share]
    for r in range(1, 16):
        arrived(pk_in.at[add_mod(share, -r, 16)], pk_rs.at[r - 1])

    def branch_value(branch):
        got = pk_in[branch]
        for i in range(1, 8):
            got = got + pk_in[2 * i + branch]
        mean = got[4:5, 0:ROWS] / D
        inv_std = lax.rsqrt(got[5:6, 0:ROWS] / D - mean * mean + EPSILON)
        return (
            inv_std * (got[0:4, 0:ROWS] - mean * got[0:4, ROWS:ROWS + 1])
            + got[0:4, ROWS + 1:ROWS + 2]
        )

    cond, uncond = branch_value(0), branch_value(1)
    guide = jnp.where(e == 0, GUIDE_HIGH, GUIDE_LOW)
    guided = uncond + guide * (cond - uncond)
    step_now = jnp.full((4, ROWS), step_ref[0], jnp.int32).astype(jnp.float32)
    delta = noise_level(1.0 - (step_now + 1.0) / STEPS) - noise_level(1.0 - step_now / STEPS)
    swap[0:4, 0:ROWS] = lat[share][0:4, :] + delta * guided
    swap_copy = remote(swap, swap_in, sw_ss, sw_rs, {"expert": 1 - e})
    swap_copy.start()
    fin[share, 0:4, 0:ROWS] = guided
    arrived(swap_in, sw_rs)
    fin[share, 4:8, 0:ROWS] = swap_in[0:4, 0:ROWS]
    fin_copies = share_copies(lambda to: fin.at[share], fin, fin_ss, fin_rs)
    for copy in fin_copies:
        copy.start()
    for r in range(1, 16):
        arrived(fin.at[add_mod(share, -r, 16)], fin_rs.at[r - 1])
    for i in range(16):
        vel_ref[4 * i:4 * i + 4, :] = fin[i, 0:4, 0:ROWS]
        rel_ref[4 * i:4 * i + 4, :] = fin[i, 4:8, 0:ROWS]

    vel_out = pltpu.make_async_copy(vel_ref, vel_hbm, out_sem.at[1])
    rel_out = pltpu.make_async_copy(rel_ref, rel_hbm, out_sem.at[2])
    vel_out.start()
    rel_out.start()

    hid_out.wait()
    for copy in msg_copies + pk_copies + fin_copies + px_copies + [swap_copy]:
        copy.wait_send()
    sent_all(v_copies + k_copies + q_copies)
    pl.when(jnp.logical_not(w_stays_mid))(w_mid_far.wait_send)
    pl.when(jnp.logical_not(w_stays))(w_far.wait_send)
    for copy in w_sent.values():
        copy.wait_send()
    for _, _, _, copy in ag_starts:
        copy.wait_send()
    for _, h, way, copy in ag_lasts:
        if ag_last(way, h):
            copy.wait_send()
        else:
            pl.when(holds)(copy.wait_send)

    @pl.when(attends)
    def _():
        def one(i, carry):
            relay(values, i, vr_ss, vr_rs).wait_send()
            relay(keys, i, kr_ss, kr_rs).wait_send()
            pl.when(jnp.logical_not(jnp.logical_and(i == z, holds)))(o_far(i).wait_send)
            return carry

        lax.fori_loop(0, 8, one, 0)
    vel_out.wait()
    rel_out.wait()


def local(
    query_raw,
    key_raw,
    value_rows,
    residual,
    latent,
    query_gain,
    key_gain,
    out_weight,
    attn_gate,
    head_shift,
    head_scale,
    head_weight,
    head_bias,
    valid_rows,
    step_index,
):
    hbm = pl.BlockSpec(memory_space=pl.ANY)
    smem = pl.BlockSpec(memory_space=pltpu.SMEM)
    dma = pltpu.SemaphoreType.DMA
    f32, bf16 = jnp.float32, jnp.bfloat16
    hidden, velocity, relayed = pl.pallas_call(
        kernel,
        out_shape=(
            jax.ShapeDtypeStruct((ROWS, WIDTH), bf16),
            jax.ShapeDtypeStruct((64, ROWS), f32),
            jax.ShapeDtypeStruct((64, ROWS), f32),
        ),
        in_specs=[hbm] * 13 + [smem] * 2,
        out_specs=(hbm, hbm, hbm),
        scratch_shapes=[
            pltpu.VMEM((ROWS, WIDTH), bf16),
            pltpu.VMEM((ROWS, WIDTH), bf16),
            pltpu.VMEM((ROWS, WIDTH), bf16),
            pltpu.VMEM((1, WIDTH), f32),
            pltpu.VMEM((1, WIDTH), f32),
            pltpu.VMEM((1, WIDTH), f32),
            pltpu.VMEM((1, WIDTH), f32),
            pltpu.VMEM((1, WIDTH), f32),
            pltpu.VMEM((64, WIDTH), bf16),
            pltpu.VMEM((1, 64), f32),
            pltpu.VMEM((64, ROWS), f32),
            pltpu.VMEM((ROWS, WIDTH), bf16),
            pltpu.VMEM((64, ROWS), f32),
            pltpu.VMEM((64, ROWS), f32),
            dma((11,)), dma((3,)),
            pltpu.VMEM((256, HD), f32),
            pltpu.VMEM((8, HD), f32),
            pltpu.VMEM((7, 8, HD), f32),
            pltpu.VMEM((ROWS, HD), f32),
            pltpu.VMEM((ROWS, HD), f32),
            pltpu.VMEM((LOCAL_HEADS, ROWS, HD), bf16),
            pltpu.VMEM((LOCAL_HEADS, ROWS, HD), bf16),
            pltpu.VMEM((TOKENS, HD), bf16),
            pltpu.VMEM((TOKENS, HD), bf16),
            pltpu.VMEM((8, ROWS, HD), bf16),
            pltpu.VMEM((1, TOKENS), f32),
            pltpu.VMEM((ROWS, TOKENS), f32),
            pltpu.VMEM((8, ROWS, HD), bf16),
            pltpu.VMEM((4, 2, ROWS, WIDTH), bf16),
            pltpu.VMEM((COLS, WIDTH), bf16),
            pltpu.VMEM((4, WIDTH, WIDTH), bf16),
            pltpu.VMEM((ROWS, WIDTH), f32),
            pltpu.VMEM((ROWS, WIDTH), bf16),
            pltpu.VMEM((ROWS, WIDTH), bf16),
            pltpu.VMEM((128, WIDTH), f32),
            pltpu.VMEM((1, HD), f32),
            pltpu.VMEM((16, 4, ROWS), f32),
            pltpu.VMEM((16, 8, 256), f32),
            pltpu.VMEM((16, 8, 256), f32),
            pltpu.VMEM((8, 256), f32),
            pltpu.VMEM((8, 256), f32),
            pltpu.VMEM((16, 8, 256), f32),
            dma((7,)), dma((7,)),
            dma((5,)), dma((8,)),
            dma((5,)), dma((8,)),
            dma((5,)), dma((8,)),
            dma((8,)), dma((8,)),
            dma((8,)), dma((8,)),
            dma((8,)), dma((2, 5)),
            dma((2, 2, 10)), dma((2, 2, 10)),
            dma, dma,
            dma, dma,
            dma((W_COPIES,)), dma((W_COPIES,)),
            dma((2,)), dma((2,)),
            dma((15,)), dma((15,)),
            dma, dma,
            dma((15,)), dma((15,)),
        ],
        compiler_params=pltpu.CompilerParams(
            collective_id=0, has_side_effects=True, vmem_limit_bytes=56 * 1024 * 1024
        ),
    )(
        query_raw[0, 0], key_raw[0, 0], value_rows[0, 0], residual[0, 0], query_gain, key_gain,
        out_weight[0].T, attn_gate, head_scale, head_shift, head_weight[0].T, head_bias,
        latent[0].T, valid_rows, step_index,
    )
    return (hidden[None, None], velocity.T[None], relayed.T[None])


def solution(mesh):
    placed = (
        P("expert", "branch", "seq", "tensor"),
        P("expert", "branch", "seq", "tensor"),
        P("expert", "branch", "seq", "tensor"),
        P("expert", "branch", "seq", "tensor"),
        P("expert", "seq", None),
        P("expert", "tensor"),
        P("expert", "tensor"),
        P("expert", "tensor", ("branch", "seq")),
        P("expert", "tensor"),
        P("expert", "tensor"),
        P("expert", "tensor"),
        P("expert", "tensor", None),
        P("expert", None),
        P("expert"),
        P("expert"),
    )
    return jax.shard_map(
        local,
        mesh=mesh,
        in_specs=placed,
        out_specs=(
            P("expert", "branch", "seq", "tensor"),
            P("expert", "seq", None),
            P("expert", "seq", None),
        ),
        check_vma=False,
    )
```
